32 devices in a mesh: fsdp: 8 (over z, y), tensor: 4 (over x, core).
Axes of the slice: x: 2, y: 2, z: 4, core: 2. Of those that a mesh axis runs over, the one named last changes fastest.
Arguments:
- inputs: bfloat16 [4096, 2048], P(('fsdp', 'tensor')), may hold values from -6 to 6
- seg_ids: int32 [4096], P('fsdp'), may hold values from 0 to 4095, as said below
- positions: int32 [4096], P('fsdp'), may hold values from 0 to 766, as said below
- w_query: bfloat16 [2048, 2048], P('fsdp', 'tensor'), may hold values from -0.125 to 0.125
- w_key: bfloat16 [2048, 2048], P('fsdp', 'tensor'), may hold values from -0.125 to 0.125
- w_value: bfloat16 [2048, 2048], P('fsdp', 'tensor'), may hold values from -0.125 to 0.125
- w_out: bfloat16 [2048, 2048], P('tensor', 'fsdp'), may hold values from -0.125 to 0.125
- query_gain: bfloat16 [16, 128], P('tensor', 'fsdp'), may hold values from 0.5 to 1.5
- key_gain: bfloat16 [16, 128], P('tensor', 'fsdp'), may hold values from 0.5 to 1.5
- attn_gain: bfloat16 [2048], P('fsdp'), may hold values from 0.5 to 1.5
- w_gate: bfloat16 [2048, 8192], P('fsdp', 'tensor'), may hold values from -0.125 to 0.125
- w_up: bfloat16 [2048, 8192], P('fsdp', 'tensor'), may hold values from -0.125 to 0.125
- w_down: bfloat16 [8192, 2048], P('tensor', 'fsdp'), may hold values from -0.0625 to 0.0625
- ffn_gain: bfloat16 [2048], P('fsdp'), may hold values from 0.5 to 1.5
- out_grad: bfloat16 [4096, 2048], P(('fsdp', 'tensor')), may hold values from -6 to 6
Outputs:
- output: bfloat16 [4096, 2048], P(('fsdp', 'tensor'))
- grad_inputs: float32 [4096, 2048], P(('fsdp', 'tensor'))
- grad_query: float32 [2048, 2048], P('fsdp', 'tensor')
- grad_key: float32 [2048, 2048], P('fsdp', 'tensor')
- grad_value: float32 [2048, 2048], P('fsdp', 'tensor')
- grad_out: float32 [2048, 2048], P('tensor', 'fsdp')
- grad_query_gain: float32 [16, 128], P('tensor', 'fsdp')
- grad_key_gain: float32 [16, 128], P('tensor', 'fsdp')
- grad_attn_gain: float32 [2048], P('fsdp')
- grad_gate: float32 [2048, 8192], P('fsdp', 'tensor')
- grad_up: float32 [2048, 8192], P('fsdp', 'tensor')
- grad_down: float32 [8192, 2048], P('tensor', 'fsdp')
- grad_ffn_gain: float32 [2048], P('fsdp')
The draws below stay inside these ranges and needn't reach their ends.
Inputs may be any that keep to these rules, and one draw needn't show every extreme that they name: seg_ids holds, for each token, the index of the first token of its sequence; no sequence crosses a block of 512 tokens of one fsdp index; each block holds one sequence longer than three quarters of it; in some block one sequence fills it; the last token of all is a sequence of its own. positions count up by one within each sequence from an offset of at most 255.
All inputs are finite; a program needn't handle non-finite values.
Results may differ from the reference program's by a relative error of at most 0.02.
Values may be sent and summed in bfloat16 or wider, within the bound.
A program may use at most 192 MiB of HBM per device.

```python
import jax
import jax.numpy as jnp
from jax import lax

D = 2048
HEADS = 16
HD = 128
FF = 8192
TOK_GRP = 512
TOKENS = 4096


def layout(key):
    groups = TOKENS // TOK_GRP
    parts = jax.random.split(key, 5)
    filled = jax.random.randint(parts[0], (), 0, groups - 1)
    group_index = jnp.arange(groups, dtype=jnp.int32)
    is_last = group_index == groups - 1
    least = 3 * TOK_GRP // 4 + 1
    length = jax.random.randint(parts[1], (groups,), least, TOK_GRP + 1)
    length = jnp.where(group_index == filled, TOK_GRP, length)
    length = jnp.where(is_last, jnp.minimum(length, TOK_GRP - 1), length)
    limit = jnp.where(is_last, TOK_GRP - 1, TOK_GRP)
    begin = jax.random.randint(parts[2], (groups,), 0, limit - length + 1)
    index = jnp.arange(TOK_GRP, dtype=jnp.int32)[None, :]
    finish = (begin + length)[:, None]
    cuts = jax.random.randint(parts[3], (groups, TOK_GRP), 0, 40) == 0
    inside = (index > begin[:, None]) & (index < finish)
    edges = (index == 0) | (index == begin[:, None]) | (index == finish)
    edges = edges | (index == TOK_GRP - 1) & is_last[:, None]
    bounds = edges | cuts & jnp.logical_not(inside)
    first_row = lax.cummax(jnp.where(bounds, index, 0), axis=1)
    seg_all = first_row + group_index[:, None] * TOK_GRP
    offsets = jax.random.randint(parts[4], (groups, TOK_GRP), 0, 256)
    offsets = jnp.where((group_index == filled)[:, None] & (index == 0), 255, offsets)
    pos_all = jnp.take_along_axis(offsets, first_row, axis=1) + index - first_row
    return (seg_all.reshape(-1).astype(jnp.int32), pos_all.reshape(-1).astype(jnp.int32))


def draw_seg_ids(key, part):
    return layout(key)[0]


def draw_positions(key, part):
    return layout(key)[1]


def shard_levels(stream_key, dims, pieces, smallest, top_value):
    level, own = 1.0, jax.random.fold_in(stream_key, 6)
    for axis_at, blocks in pieces:
        heights = jnp.exp(jax.random.uniform(jax.random.fold_in(own, axis_at), (blocks,), jnp.float32, smallest / len(pieces), top_value / len(pieces)))
        level = level * jnp.repeat(heights, dims[axis_at] // blocks).reshape([-1 if axis == axis_at else 1 for axis in range(len(dims))])
    return level


def noise(own_key, dims, deviation, most, shards=(), kind=jnp.bfloat16):
    entries = deviation * jax.random.normal(own_key, dims, jnp.float32)
    if shards:
        entries = entries * shard_levels(own_key, dims, shards, -0.22, 0.18)
    return jnp.clip(entries, -most, most).astype(kind)


def setup_inputs(seed: int = 0) -> dict:
    seeds = jax.random.split(jax.random.key(seed), 16)
    inputs = noise(seeds[0], (TOKENS, D), 1.0, 6.0, ((0, 32),))
    seg_ids = draw_seg_ids(jax.random.fold_in(seeds[15], 71), 0)
    positions = draw_positions(jax.random.fold_in(seeds[15], 71), 0)
    w_query = noise(seeds[3], (D, D), D ** -0.5, 0.125, ((0, 8), (1, 4)))
    w_key = noise(seeds[4], (D, D), D ** -0.5, 0.125, ((0, 8), (1, 4)))
    w_value = noise(seeds[5], (D, D), D ** -0.5, 0.125, ((0, 8), (1, 4)))
    w_out = noise(seeds[6], (D, D), D ** -0.5, 0.125, ((0, 4), (1, 8)))
    query_gain = jnp.clip(1.0 + 0.1 * jax.random.normal(seeds[7], (HEADS, HD), jnp.float32), 0.5, 1.5).astype(jnp.bfloat16)
    key_gain = jnp.clip(1.0 + 0.1 * jax.random.normal(seeds[8], (HEADS, HD), jnp.float32), 0.5, 1.5).astype(jnp.bfloat16)
    attn_gain = jnp.clip(1.0 + 0.1 * jax.random.normal(seeds[9], (D,), jnp.float32), 0.5, 1.5).astype(jnp.bfloat16)
    w_gate = noise(seeds[10], (D, FF), D ** -0.5, 0.125, ((0, 8), (1, 4)))
    w_up = noise(seeds[11], (D, FF), D ** -0.5, 0.125, ((0, 8), (1, 4)))
    w_down = noise(seeds[12], (FF, D), FF ** -0.5, 0.0625, ((0, 4), (1, 8)))
    ffn_gain = jnp.clip(1.0 + 0.1 * jax.random.normal(seeds[13], (D,), jnp.float32), 0.5, 1.5).astype(jnp.bfloat16)
    out_grad = noise(seeds[14], (TOKENS, D), 1.0, 6.0, ((0, 32),))
    return {"inputs": inputs, "seg_ids": seg_ids, "positions": positions, "w_query": w_query, "w_key": w_key, "w_value": w_value, "w_out": w_out, "query_gain": query_gain, "key_gain": key_gain, "attn_gain": attn_gain, "w_gate": w_gate, "w_up": w_up, "w_down": w_down, "ffn_gain": ffn_gain, "out_grad": out_grad}


NORM_EPS = 1e-06
ROPE_THETA = 500000.0

@jax.custom_vjp
def low(v):
    return lax.optimization_barrier(v.astype(jnp.bfloat16)).astype(jnp.float32)

@jax.custom_vjp
def low_back(v):
    return v

def low_keep(v):
    return (low(v), None)

def low_pass(kept, grad):
    return (grad,)

def back_keep(v):
    return (v, None)

def back_low(kept, grad):
    return (low(grad),)
low.defvjp(low_keep, low_pass)
low_back.defvjp(back_keep, back_low)

def rope_tables(positions, head_size):
    half_size = head_size // 2
    freq = ROPE_THETA ** (-(jnp.arange(half_size, dtype=jnp.float32) * 2.0) / head_size)
    angle = positions.astype(jnp.float32)[:, None] * freq[None, :]
    return (jnp.cos(angle), jnp.sin(angle))

def rotate(values, cosine, sine):
    half_size = values.shape[-1] // 2
    first = values[..., :half_size]
    second = values[..., half_size:]
    cosine = cosine[:, None, :]
    sine = sine[:, None, :]
    return jnp.concatenate([first * cosine - second * sine, second * cosine + first * sine], axis=-1)

def rms_norm(values, gain):
    inverse = lax.rsqrt(lax.optimization_barrier(jnp.mean(values * values, axis=1, keepdims=True)) + NORM_EPS)
    return values * inverse * gain

def layer_group(inputs, seg_ids, positions, w_query, w_key, w_value, w_out, query_gain, key_gain, attn_gain, w_gate, w_up, w_down, ffn_gain):
    highest = lax.Precision.HIGHEST
    row_count = inputs.shape[0]
    query_raw = low_back(jnp.dot(inputs, w_query, precision=highest))
    key_raw = low_back(jnp.dot(inputs, w_key, precision=highest))
    value_raw = low_back(jnp.dot(inputs, w_value, precision=highest))
    query_norm = rms_norm(query_raw, query_gain.reshape(-1))
    key_norm = rms_norm(key_raw, key_gain.reshape(-1))
    cosine, sine = rope_tables(positions, HD)
    query_rot = low(rotate(query_norm.reshape(row_count, HEADS, HD), cosine, sine))
    key_rot = low(rotate(key_norm.reshape(row_count, HEADS, HD), cosine, sine))
    value_low = low(value_raw).reshape(row_count, HEADS, HD)
    scores = jnp.einsum('qhd,khd->hqk', query_rot, key_rot, precision=highest) * HD ** (-0.5)
    scores = low_back(scores)
    row_index = jnp.arange(row_count, dtype=jnp.int32)
    allowed = (seg_ids[:, None] == seg_ids[None, :]) & (row_index[None, :] <= row_index[:, None])
    scores = jnp.where(allowed[None], scores, -1e+30)
    probs = jax.nn.softmax(scores, axis=-1)
    mixed = jnp.einsum('hqk,khd->qhd', low(probs), value_low, precision=highest).reshape(row_count, -1)
    mixed = low_back(low(mixed))
    attn_raw = low_back(jnp.dot(mixed, w_out, precision=highest))
    resid = inputs + rms_norm(attn_raw, attn_gain)
    resid_low = low(resid)
    gate_raw = low_back(jnp.dot(resid_low, w_gate, precision=highest))
    up_raw = low_back(jnp.dot(resid_low, w_up, precision=highest))
    hidden = low(jax.nn.silu(gate_raw) * up_raw)
    ffn_raw = low_back(jnp.dot(hidden, w_down, precision=highest))
    return resid + rms_norm(ffn_raw, ffn_gain)

def reference(inputs, seg_ids, positions, w_query, w_key, w_value, w_out, query_gain, key_gain, attn_gain, w_gate, w_up, w_down, ffn_gain, out_grad):
    groups = inputs.shape[0] // TOK_GRP

    def forward(x_all, wq_all, wk_all, wv_all, wo_all, gq_all, gk_all, ga_all, wg_all, wu_all, wd_all, gf_all):

        def one_group(packed):
            return layer_group(packed[0], packed[1], packed[2], wq_all, wk_all, wv_all, wo_all, gq_all, gk_all, ga_all, wg_all, wu_all, wd_all, gf_all)
        stacked = lax.map(jax.checkpoint(one_group), (x_all.reshape(groups, TOK_GRP, -1), seg_ids.reshape(groups, TOK_GRP), positions.reshape(groups, TOK_GRP)))
        return stacked.reshape(x_all.shape)
    floats = [a.astype(jnp.float32) for a in (inputs, w_query, w_key, w_value, w_out, query_gain, key_gain, attn_gain, w_gate, w_up, w_down, ffn_gain)]
    result, pull_back = jax.vjp(forward, *floats)
    grads = pull_back(out_grad.astype(jnp.float32))
    return (result.astype(jnp.bfloat16), grads[0], grads[1], grads[2], grads[3], grads[4], grads[5], grads[6], grads[7], grads[8], grads[9], grads[10], grads[11])
```

```python
import functools

import jax
import jax.numpy as jnp
import numpy as np
from jax import lax
from jax.experimental import pallas as pl
from jax.experimental.pallas import tpu as pltpu
from jax.sharding import PartitionSpec as P

HD = 128
NORM_EPS = 1e-06
ROPE_THETA = 500000.0
BF = jnp.bfloat16
F32 = jnp.float32
MIB = 1 << 20


class Place:
    def __init__(self, count):
        self.count = count
        self.outers = count // 4
        self.index = lax.axis_index("fsdp")
        self.tensor = lax.axis_index("tensor")
        self.low = self.index % 2
        self.high = self.index // 2
        self.pair = self.high % 2
        self.outer = self.high // 2
        self.core = self.tensor % 2
        self.side = self.tensor // 2

    def device(self, outer, pair, low, core, side):
        return {"fsdp": (outer * 2 + pair) * 2 + low, "tensor": side * 2 + core}

    def peer(self, pair=0, core=0, side=0):
        return self.device(
            self.outer, flip(self.pair, pair), self.low, flip(self.core, core), flip(self.side, side)
        )

    def slot(self, pair=0, core=0, side=0):
        return flip(self.pair, pair) * 4 + flip(self.core, core) * 2 + flip(self.side, side)

    def line(self, step, pair):
        outer = (self.outer + step) % self.outers
        return self.device(outer, flip(self.pair, pair), self.low, self.core, self.side)

    def high_at(self, step, pair):
        return ((self.outer + step + self.outers) % self.outers) * 2 + flip(self.pair, pair)

    def across(self):
        return self.device(self.outer, self.pair, 1 - self.low, self.core, self.side)

    def lines(self):
        return line_kinds(self.count)

    def group(self):
        return [(p, c, s) for p in (0, 1) for c in (0, 1) for s in (0, 1) if p or c or s]


def line_kinds(count):
    return [(step, pair) for step in reversed(range(count // 4)) for pair in (0, 1) if step or pair]


def flip(bit, yes):
    return 1 - bit if yes else bit


def greet(devices):
    barrier = pltpu.get_barrier_semaphore()
    for device in devices:
        pl.semaphore_signal(barrier, inc=1, device_id=device, device_id_type=pl.DeviceIdType.MESH)
    pl.semaphore_wait(barrier, len(devices))


def send(src, dst, sends, recvs, slot, device):
    return pltpu.make_async_remote_copy(
        src_ref=src,
        dst_ref=dst,
        send_sem=sends.at[slot],
        recv_sem=recvs.at[slot],
        device_id=device,
        device_id_type=pl.DeviceIdType.MESH,
    )


def product(left, right):
    return lax.dot_general(left, right, (((1,), (0,)), ((), ())), preferred_element_type=F32)


def product_last(left, right):
    return lax.dot_general(left, right, (((1,), (1,)), ((), ())), preferred_element_type=F32)


def product_first(left, right):
    return lax.dot_general(left, right, (((0,), (0,)), ((), ())), preferred_element_type=F32)


class Gather:
    slots = 9

    def __init__(self, place, rows, sends, recvs, split=False):
        half = rows.shape[1] // 2

        def go(slot, device, part=None, **kw):
            ref = rows.at[place.slot(**kw)]
            if part is not None:
                ref = rows.at[place.slot(**kw), pl.ds(part * half, half)]
            return send(ref, ref, sends, recvs, slot, place.peer(**device))

        self.to_pair = go(0, dict(pair=1))
        self.to_side = go(1, dict(side=1))
        self.to_core = go(2, dict(core=1))
        self.pair_to_core = go(5, dict(core=1), pair=1)
        self.side_to_core = go(6, dict(core=1), side=1)
        if split:
            self.relays = [go(3, dict(side=1), 0, pair=1), go(4, dict(pair=1), 1, side=1)]
            self.last = [go(7, dict(core=1), 0, pair=1, side=1), go(8, dict(core=1), 1, pair=1, side=1)]
        else:
            self.relays = [go(3, dict(side=1), pair=1)]
            self.last = [go(7, dict(core=1), pair=1, side=1)]

    def start(self):
        self.to_pair.start()
        self.to_side.start()
        self.to_core.start()

    def relay(self):
        self.to_pair.wait_recv()
        self.relays[0].start()
        self.pair_to_core.start()
        self.to_side.wait_recv()
        for copy in self.relays[1:]:
            copy.start()
        self.side_to_core.start()

    def finish(self):
        for relay, copy in zip(self.relays, self.last):
            relay.wait_recv()
            copy.start()
        for copy in [self.to_core, self.pair_to_core, self.side_to_core] + self.last:
            copy.wait_recv()

    def drain(self):
        for copy in [self.to_pair, self.to_side, self.to_core, self.pair_to_core, self.side_to_core]:
            copy.wait_send()
        for copy in self.relays + self.last:
            copy.wait_send()


class Scatter:
    order = [(1, 1), (1, 0), (0, 1), (0, 0)]

    def __init__(self, place, tile, parts, from_core, from_chips, total, sends, recvs, via=False):
        self.place, self.tile, self.parts = place, tile, parts
        self.from_core, self.from_chips, self.total, self.via = from_core, from_chips, total, via
        self.to_core = [
            send(
                parts.at[place.slot(pair=pair, core=1, side=side)],
                from_core.at[slot],
                sends,
                recvs,
                slot,
                place.peer(core=1),
            )
            for slot, (pair, side) in enumerate(self.order)
        ]
        self.to_chips = [
            send(
                parts.at[place.slot(pair=pair, side=side)],
                from_chips.at[slot],
                sends,
                recvs,
                4 + slot,
                place.peer(pair=pair if slot or not via else 0, side=side),
            )
            for slot, (pair, side) in enumerate(self.order[:3])
        ]

    def first(self, pair):
        place = self.place
        self.tile(flip(place.pair, pair), 1 - place.core)
        for slot, (p, side) in enumerate(self.order):
            if p == pair:
                self.to_core[slot].start()

    def both(self, slot):
        pair, side = self.order[slot]
        mine = self.place.slot(pair=pair, side=side)
        return mine, self.parts[mine].astype(F32) + self.from_core[slot].astype(F32)

    def second(self, pair):
        self.tile(flip(self.place.pair, pair), self.place.core)
        for slot, (p, side) in enumerate(self.order):
            if p != pair:
                continue
            self.to_core[slot].wait_recv()
            if self.via and slot == 1:
                continue
            mine, both = self.both(slot)
            if slot < 3:
                self.parts[mine] = both.astype(BF)
                self.to_chips[slot].start()
            else:
                self.total[...] = both

    def relay(self):
        if self.via:
            self.to_chips[0].wait_recv()
            mine, both = self.both(1)
            self.parts[mine] = (both + self.from_chips[0].astype(F32)).astype(BF)
            self.to_chips[1].start()

    def third(self):
        for slot, copy in enumerate(self.to_chips):
            if slot or not self.via:
                copy.wait_recv()
                self.total[...] += self.from_chips[slot].astype(F32)

    def drain(self):
        for copy in self.to_core + self.to_chips:
            copy.wait_send()


def tiles(left_ref, right, parts, lanes):
    own, width = parts.shape[1:]

    def tile(pair, core):
        first = pair * 4 + core * 2
        m = pl.ds(pl.multiple_of(first * own, 2 * own), 2 * own)

        @pl.loop(0, width // 256)
        def _(n):
            at = pl.ds(pl.multiple_of(n * 256, 256), 256)
            out = product_last(left_ref[m, :], right[at, lanes]).astype(BF)
            parts[first, :, at] = out[:own]
            parts[first + 1, :, at] = out[own:]

    return tile


def exchange_sums(place, stats, columns, sends, recvs):
    tokens = stats.shape[2]
    mine = place.slot()
    rows = [jnp.transpose(jnp.broadcast_to(column, (tokens, 128)))[0:1] for column in columns]
    stats[mine] = jnp.concatenate(rows + [jnp.zeros((6, tokens), F32)], axis=0)
    copies = []
    for i, (p, c, s) in enumerate(place.group()):
        copy = send(stats.at[mine], stats.at[mine], sends, recvs, i, place.peer(p, c, s))
        copy.start()
        copies.append(copy)
    return copies


def finish_sums(stats, copies):
    for copy in copies:
        copy.wait_recv()
    sums = stats[0]
    for g in range(1, 8):
        sums = sums + stats[g]
    return sums


def over_lanes(row):
    return jnp.transpose(jnp.broadcast_to(row, (128, row.shape[1])))


class Stream:
    def __init__(self, place, sources, full, sends, recvs, held, local):
        self.place = place
        self.kinds = sorted(place.lines())
        self.lines, self.over, self.hold, self.keep = [], [], [], []
        self.next = self.begun = self.begun_over = 0
        self.ahead, self.over_ahead = 1, 8
        depth = full.shape[1] // place.count
        per = place.count - 1
        for i, source in enumerate(sources):
            def rows(high, low, i=i):
                at = (high * 2 + low) * depth
                return full.at[i, pl.ds(pl.multiple_of(at, depth), depth)]

            own = rows(place.high, place.low)
            first = i * per
            self.lines.append(
                [
                    send(source(flip(place.pair, pair)), own, sends, recvs, first + k, place.line(step, pair))
                    for k, (step, pair) in enumerate(self.kinds)
                ]
            )
            first += len(self.kinds)
            over = [send(source(place.pair), own, sends, recvs, first, place.across())]
            for k, (step, pair) in enumerate(self.kinds):
                block = rows(place.high_at(-step, pair), place.low)
                over.append(send(block, block, sends, recvs, first + 1 + k, place.across()))
            self.over.append(over)
            self.hold.append(pltpu.make_async_copy(source(place.pair), held.at[i], local.at[0, i]))
            self.keep.append(pltpu.make_async_copy(held.at[i], own, local.at[1, i]))

    def place_own(self):
        for copy in self.hold:
            copy.start()
        for hold, keep in zip(self.hold, self.keep):
            hold.wait()
            keep.start()

    def fill(self):
        while self.begun < min(self.next // len(self.kinds) + self.ahead, len(self.lines)):
            for copy in self.lines[self.begun]:
                copy.start()
            self.begun += 1
        while self.begun_over < min(self.next // len(self.kinds) + self.over_ahead, len(self.lines)):
            self.over[self.begun_over][0].start()
            self.begun_over += 1

    def pump(self, number=1):
        per = len(self.kinds)
        for _ in range(number):
            i, k = divmod(self.next, per)
            if i >= len(self.lines):
                return
            self.lines[i][k].wait_recv()
            self.over[i][k + 1].start()
            self.next += 1
            if self.next % per == 0:
                self.fill()

    def arrive(self, i):
        self.pump(max(0, (i + 1) * len(self.kinds) - self.next))
        for copy in self.over[i]:
            copy.wait_recv()
        self.keep[i].wait()

    def drain(self):
        for copies in self.lines + self.over:
            for copy in copies:
                copy.wait_send()


ANY = pl.BlockSpec(memory_space=pl.ANY)
VMEM = pl.BlockSpec(memory_space=pltpu.VMEM)
DMA = pltpu.SemaphoreType.DMA


FORWARD_ORDER = (
    "k", "k", "k", "k", "k", "k", "xr", "k", "w2", "k", "xf", "t", "k", "k", "t", "k", "t", "q0",
    "k", "k", "q1", "q2", "s", "k", "k", "sf", "rope", "k", "k", "k", "k", "a", "a", "k", "k", "k",
    "k", "t", "f", "s1", "k", "k", "k", "k", "k", "s0", "rl", "k", "T", "k", "N", "k", "k", "R",
    "k", "k", "k", "k", "k", "G", "t", "g0", "k", "k", "k", "k", "g1", "t", "k", "k", "w2", "g2",
    "k", "k", "k", "t", "g3", "k", "t", "k", "t", "t",
)


def forward_kernel(
    count,
    rows_ref, q_ref, k_ref, v_ref, o_ref, gate_ref, up_ref, down_ref, gains_ref, tokens_ref, angles_ref, top_ref,
    full, gains_out, q_rot_out, k_rot_out, v_low_out, q_hat_out, k_hat_out, inv_out,
    normed_out, ainv_out, gate_out, up_out, output, part_out, probs_out, cos_out, sin_out, grad_out, mixed_turned, hidden_turned,
    rows_turned, mid_turned,
    all_rows, all_gains, gains, own_rows, att_w, ffn_w, raw, q_rot, k_rot, v_low, q_hat, k_hat, inv_ref,
    normed_ref, ainv_ref, gate_act, up_act, result, part_gain, probs_ref, cos_ref, sin_ref, mixed_t,
    bias_ref, token_rows, o_turned, down_turned, held,
    mixed, mid, hidden, turning, resid_ref, stats, parts, from_core, from_chips, total,
    wsends, wrecvs, keeps, loads, flushes, xsends, xrecvs, nsends, nrecvs, ssends, srecvs,
    rsends, rrecvs, gsends, grecvs, r2sends, r2recvs, g2sends, g2recvs, turn_sems, tsends, trecvs,
):
    place = Place(count)
    own, width = rows_ref.shape
    tokens = 8 * own
    big = tokens // 2
    cols = q_ref.shape[1] // 2
    heads = cols // HD
    mine = place.slot()
    others = [(place.index + step) % count for step in range(1, count)]

    first_copies = [
        pltpu.make_async_copy(rows_ref, all_rows.at[mine], loads.at[0]),
        pltpu.make_async_copy(gains_ref, all_gains.at[place.index], loads.at[1]),
        pltpu.make_async_copy(rows_ref, own_rows, loads.at[2]),
    ]
    for copy in first_copies:
        copy.start()
    turn_here = o_turned.shape[0] % 128 == 0
    if turn_here:
        narrow = [
            pltpu.make_async_copy(o_ref, ffn_w.at[pl.ds(0, o_ref.shape[0]), pl.ds(cols, cols)], loads.at[3]),
            pltpu.make_async_copy(down_ref, ffn_w.at[pl.ds(0, down_ref.shape[0]), pl.ds(0, cols)], loads.at[4]),
        ]
        for copy in narrow:
            copy.start()
    blocks = [side * 2 + core for core in (0, 1) for side in (0, 1)]
    token_rows[place.pair] = jnp.concatenate(
        [tokens_ref[:, block * own : (block + 1) * own] for block in blocks], axis=1
    )
    greet(
        [{"fsdp": other, "tensor": place.tensor} for other in others]
        + [place.peer(p, c, s) for p, c, s in place.group() if c or s]
    )
    token_copy = send(
        token_rows.at[place.pair], token_rows.at[place.pair], tsends, trecvs, 0, place.peer(pair=1)
    )
    token_copy.start()

    def pieces(ref):
        half = ref.shape[1] // 2

        def source(j):
            return lambda h: ref.at[:, pl.ds(pl.multiple_of(h * half + j * cols, cols), cols)]

        return [source(j) for j in range(half // cols)]

    o_source, down_source = (o_turned, down_turned) if turn_here else (o_ref, down_ref)
    gate_pieces, up_pieces = pieces(gate_ref), pieces(up_ref)
    sources = [pieces(ref)[0] for ref in (q_ref, k_ref, v_ref, o_source)]
    for pair in zip(gate_pieces, up_pieces):
        sources.extend(pair)
    sources.extend(pieces(down_source))
    steps = len(gate_pieces)
    stream = Stream(place, sources, full, wsends, wrecvs, held, keeps)
    rows_gather = Gather(place, all_rows, xsends, xrecvs)
    first_copies[0].wait()
    rows_gather.start()
    if turn_here:
        narrow[0].wait()
        o_turned[...] = jnp.transpose(ffn_w[: o_ref.shape[0], cols : 2 * cols])
        narrow[1].wait()
        for block in range(down_ref.shape[0] // 512):
            at = slice(block * 512, (block + 1) * 512)
            down_turned[:, at] = jnp.transpose(ffn_w[at, :cols])
    stream.fill()
    stream.place_own()
    first_copies[1].wait()
    gain_copies = []
    for i, other in enumerate(others):
        copy = send(
            all_gains.at[place.index],
            all_gains.at[place.index],
            nsends,
            nrecvs,
            i,
            {"fsdp": other, "tensor": place.tensor},
        )
        copy.start()
        gain_copies.append(copy)

    flushed = []

    def flush(src, dst):
        copy = pltpu.make_async_copy(src, dst, flushes.at[len(flushed)])
        copy.start()
        flushed.append(copy)

    token_copy.wait_recv()
    row = lax.broadcasted_iota(jnp.int32, (big, 128), 0)
    natural = row // own % 2 * (2 * own) + row // (2 * own) * own + row % own
    lane = lax.broadcasted_iota(jnp.int32, (big, 128), 1)
    for block in range(2):
        at = slice(block * big, (block + 1) * big)
        angle = over_lanes(token_rows[block, 0:1]) * angles_ref[0:1]
        cos_ref[at] = jnp.cos(angle)
        sin_ref[at] = jnp.sin(angle) * angles_ref[1:2]
        starts = over_lanes(token_rows[block, 1:2])
        for c in range(big // 128):
            lanes = slice(c * 128, (c + 1) * 128)
            first = c * 128
            key = first // own % 2 * (2 * own) + first // (2 * own) * own + first % own + lane
            allowed = (starts == token_rows[block, 1:2, lanes]) & (key <= natural)
            bias_ref[block, :, lanes] = jnp.where(allowed, 0.0, -1e30).astype(BF)
    flush(cos_ref, cos_out)
    flush(sin_ref, sin_out)

    turns = [(all_rows, rows_turned, block) for block in range(width // 512)]
    turns += [(mid, mid_turned, block) for block in range(width // 512)]
    turns += [(hidden, hidden_turned, block) for block in range(hidden.shape[1] // 512)]
    turned_copies = []

    def turn():
        n = len(turned_copies)
        ref, target, block = turns[n]
        if n >= 2:
            turned_copies[-2].wait()
        at = slice(block * 512, (block + 1) * 512)
        part = ref[:, :, at].reshape(tokens, 512) if len(ref.shape) == 3 else ref[:, at]
        turning[n % 2] = jnp.transpose(part)
        copy = pltpu.make_async_copy(turning.at[n % 2], target.at[at], turn_sems.at[n])
        copy.start()
        turned_copies.append(copy)

    def load(i, into):
        stream.arrive(i)
        copy = pltpu.make_async_copy(full.at[i], into, loads.at[5 + i])
        copy.start()
        return copy

    lanes_of = lambda c, number=1: pl.ds(c * cols, number * cols)
    wide = width // gains.shape[1]
    gain_row = lambda first: jnp.concatenate([gains[r : r + 1] for r in range(first, first + wide)], axis=1)

    def rows_arrive():
        rows_gather.finish()
        for copy in gain_copies:
            copy.wait_recv()
        sums = all_gains[0].astype(F32)
        for f in range(1, count):
            sums = sums + all_gains[f].astype(F32)
        gains[...] = sums
        flush(gains, gains_out)

    def project(which):
        load(which, att_w.at[:, lanes_of(which)]).wait()

        @pl.loop(0, 4)
        def _(i):
            m = pl.ds(pl.multiple_of(i * 2 * own, 2 * own), 2 * own)
            left = all_rows[pl.ds(i * 2, 2)].reshape(2 * own, width)
            raw[m, lanes_of(which)] = product(left, att_w[:, lanes_of(which)])

    sum_copies = []

    def squares():
        parts_of = [raw[:, at : at + cols] for at in (0, cols)]
        parts_of = [jnp.sum(part * part, axis=1, keepdims=True) for part in parts_of]
        sum_copies.extend(exchange_sums(place, stats, parts_of, ssends, srecvs))
        v_low[...] = raw[:, 2 * cols :].astype(BF)
        flush(v_low, v_low_out)

    def inverses():
        inverse = lax.rsqrt(finish_sums(stats, sum_copies) / width + NORM_EPS)
        inv_ref[0] = over_lanes(inverse[0:1])
        inv_ref[1] = over_lanes(inverse[1:2])
        flush(inv_ref, inv_out)

    def rotate():
        gain_at = pl.ds(pl.multiple_of(place.pair * cols, cols), cols)

        @pl.loop(0, 8)
        def _(i):
            m = pl.ds(pl.multiple_of(i * own, own), own)
            cosine = cos_ref[m]
            sine = sin_ref[m]
            for which, hat, rot in ((0, q_hat, q_rot), (1, k_hat, k_rot)):
                inv = inv_ref[which, m]
                gain = gains[2 * wide + which : 2 * wide + which + 1, gain_at]
                for h in range(heads):
                    lanes = slice(h * HD, (h + 1) * HD)
                    value = raw[m, which * cols + h * HD : which * cols + (h + 1) * HD] * inv
                    hat[m, lanes] = value
                    value = value * gain[:, lanes]
                    value = value * cosine + pltpu.roll(value, HD // 2, 1) * sine
                    rot[m, lanes] = value.astype(BF)

        for src, dst in ((q_rot, q_rot_out), (k_rot, k_rot_out), (q_hat, q_hat_out), (k_hat, k_hat_out)):
            flush(src, dst)

    scale = HD ** (-0.5)
    quarter = big // 2

    def attend(block, i):
        h = i // 2
        lanes = pl.ds(pl.multiple_of(h * HD, HD), HD)
        q_at = pl.ds(pl.multiple_of(block * big + i % 2 * quarter, quarter), quarter)
        k_at = pl.ds(pl.multiple_of(block * big, big), big)
        b_at = pl.ds(pl.multiple_of(i % 2 * quarter, quarter), quarter)
        scores = product_last(q_rot[q_at, lanes], k_rot[k_at, lanes]) * scale + bias_ref[block, b_at].astype(F32)
        top = jnp.max(scores, axis=1, keepdims=True)
        grown = jnp.exp(scores - top)
        probs = grown / jnp.sum(grown, axis=1, keepdims=True)
        probs = probs.astype(BF)
        probs_ref[block * heads + h, b_at] = probs
        mixed[q_at, lanes] = product(probs, v_low[k_at, lanes]).astype(BF)

    attended = [0]

    def attention():
        pl.loop(0, 2 * heads)(functools.partial(attend, attended[0]))
        attended[0] += 1

    tile = tiles(mixed, att_w, parts, lanes_of(3))
    scatter = Scatter(place, tile, parts, from_core, from_chips, total, rsends, rrecvs, via=True)
    gather = Gather(place, mid, gsends, grecvs)

    def out_first():
        out_load = load(3, att_w.at[:, lanes_of(3)])
        mixed_t[...] = jnp.transpose(mixed[...])
        flush(mixed_t, mixed_turned)
        flush(probs_ref, probs_out)
        rows_gather.drain()
        out_load.wait()
        scatter.first(1)
        scatter.first(0)

    def norm():
        araw = total[...]
        inv = lax.rsqrt(jnp.mean(araw * araw, axis=1, keepdims=True) + NORM_EPS)
        normed = araw * inv
        normed_ref[...] = normed
        ainv_ref[...] = jnp.broadcast_to(inv, (own, 128))
        first_copies[2].wait()
        resid = own_rows[...].astype(F32) + normed * gain_row(0)
        resid_ref[...] = resid
        mid[mine] = resid.astype(BF)
        gather.start()
        for src, dst in ((normed_ref, normed_out), (ainv_ref, ainv_out)):
            flush(src, dst)

    loaded = {}

    def load_step(j):
        if j < steps and j not in loaded:
            at = j % 2 * 2
            loaded[j] = [load(4 + 2 * j + r, ffn_w.at[:, lanes_of(at + r)]) for r in range(2)]

    def gate_and_up(j):
        load_step(j)
        for copy in loaded[j]:
            copy.wait()
        n = slice(j * cols, (j + 1) * cols)

        @pl.loop(0, 4)
        def _(i):
            m = pl.ds(pl.multiple_of(i * 2 * own, 2 * own), 2 * own)
            left = mid[pl.ds(i * 2, 2)].reshape(2 * own, width)
            both = product(left, ffn_w[:, lanes_of(j % 2 * 2, 2)])
            gate = both[:, :cols]
            up = both[:, cols:]
            sig = jax.nn.sigmoid(gate)
            silu = gate * sig
            gate_act[m, n] = up * sig * (1.0 + gate * (1.0 - sig))
            up_act[m, n] = silu
            hidden[m, n] = (silu * up).astype(BF)

        if j == steps - 1:
            for src, dst in ((gate_act, gate_out), (up_act, up_out)):
                flush(src, dst)

    actions = {
        "k": stream.pump,
        "t": turn,
        "xr": rows_gather.relay,
        "xf": rows_arrive,
        "q0": lambda: project(0),
        "q1": lambda: project(1),
        "q2": lambda: project(2),
        "s": squares,
        "sf": inverses,
        "rope": rotate,
        "a": attention,
        "f": out_first,
        "s1": lambda: scatter.second(1),
        "s0": lambda: scatter.second(0),
        "rl": scatter.relay,
        "T": scatter.third,
        "N": norm,
        "R": gather.relay,
        "G": gather.finish,
    }
    for j in range(steps):
        actions["g%d" % j] = functools.partial(gate_and_up, j)
    each = len(stream.kinds) // 3
    for name in FORWARD_ORDER:
        if name == "k":
            stream.pump(each)
        elif name[0] == "w":
            stream.ahead = int(name[1:])
            stream.fill()
        else:
            actions[name]()

    downs = [
        load(i, att_w.at[:, lanes_of(j)]) for j, i in enumerate(range(4 + 2 * steps, len(sources)))
    ]
    for copy in downs:
        copy.wait()
    scatter.drain()
    tile = tiles(hidden, att_w, parts, lanes_of(0, steps))
    again = Scatter(place, tile, parts, from_core, from_chips, total, r2sends, r2recvs)
    again.first(1)
    again.first(0)
    again.second(1)
    again.second(0)
    top = top_ref[...].astype(F32)
    gain = gain_row(wide)
    again.third()
    fraw = total[...]
    inv = lax.rsqrt(jnp.mean(fraw * fraw, axis=1, keepdims=True) + NORM_EPS)
    normed = fraw * inv
    scaled = top * gain
    inner = jnp.mean(scaled * normed, axis=1, keepdims=True)
    all_rows[mine] = (inv * (scaled - normed * inner)).astype(BF)
    last = Gather(place, all_rows, g2sends, g2recvs, split=True)
    last.start()
    result[...] = (resid_ref[...] + normed * gain).astype(BF)
    part_gain[...] = jnp.broadcast_to(jnp.sum(top * normed, axis=0, keepdims=True), part_gain.shape)
    flush(result, output)
    flush(part_gain, part_out)
    last.relay()
    stream.drain()
    gather.drain()
    again.drain()
    for copy in sum_copies + gain_copies + [token_copy]:
        copy.wait_send()
    last.finish()
    flush(all_rows, grad_out)
    last.drain()
    for copy in flushed + turned_copies[-2:]:
        copy.wait()


def run_forward(count, rows, wq, wk, wv, wo, gate, up, down, gains, token_rows, angles, top):
    own, width = rows.shape
    tokens = 8 * own
    half = gate.shape[1] // 2
    cols = wq.shape[1] // 2
    depth = width // count
    pieces = 4 + 3 * (half // cols)
    per = pieces * (count - 1)
    shape = jax.ShapeDtypeStruct
    outs = (
        shape((pieces, width, cols), BF),
        shape(gains.shape, F32),
        shape((tokens, cols), BF), shape((tokens, cols), BF), shape((tokens, cols), BF),
        shape((tokens, cols), F32), shape((tokens, cols), F32), shape((2, tokens, 128), F32),
        shape((own, width), F32), shape((own, 128), F32),
        shape((tokens, half), F32), shape((tokens, half), F32),
        shape((own, width), BF), shape((8, width), F32), shape((2 * cols // HD, tokens // 2, tokens // 2), BF),
        shape((tokens, 128), F32), shape((tokens, 128), F32),
        shape((8, own, width), BF),
        shape((cols, tokens), BF), shape((half, tokens), BF), shape((width, tokens), BF), shape((width, tokens), BF),
    )
    scratch = lambda out: pltpu.VMEM(out.shape, out.dtype)
    return pl.pallas_call(
        functools.partial(forward_kernel, count),
        out_shape=outs,
        in_specs=[ANY] * 9 + [VMEM] * 3,
        out_specs=[ANY] * len(outs),
        scratch_shapes=[
            pltpu.VMEM((8, own, width), BF),
            pltpu.VMEM((count,) + gains.shape, BF),
            scratch(outs[1]),
            pltpu.VMEM((own, width), BF),
            pltpu.VMEM((width, max(4 * cols, half)), BF),
            pltpu.VMEM((width, 4 * cols), BF),
            pltpu.VMEM((tokens, 3 * cols), F32),
            *[scratch(out) for out in outs[2:-5]],
            scratch(outs[-4]),
            pltpu.VMEM((2, tokens // 2, tokens // 2), BF),
            pltpu.VMEM((2,) + token_rows.shape, F32),
            pltpu.VMEM((depth, 2 * cols), BF),
            pltpu.VMEM((depth, 2 * half), BF),
            pltpu.VMEM((pieces, depth, cols), BF),
            pltpu.VMEM((tokens, cols), BF),
            pltpu.VMEM((8, own, width), BF),
            pltpu.VMEM((tokens, half), BF),
            pltpu.VMEM((2, 512, tokens), BF),
            pltpu.VMEM((own, width), F32),
            pltpu.VMEM((8, 8, tokens), F32),
            pltpu.VMEM((8, own, width), BF),
            pltpu.VMEM((4, own, width), BF),
            pltpu.VMEM((3, own, width), BF),
            pltpu.VMEM((own, width), F32),
            DMA((per,)), DMA((per,)), DMA((2, pieces)), DMA((5 + pieces,)), DMA((len(outs),)),
            DMA((9,)), DMA((9,)),
            DMA((count - 1,)), DMA((count - 1,)),
            DMA((7,)), DMA((7,)),
            DMA((7,)), DMA((7,)),
            DMA((9,)), DMA((9,)),
            DMA((7,)), DMA((7,)),
            DMA((9,)), DMA((9,)),
            DMA((2 * (width // 512) + half // 512,)),
            DMA((1,)), DMA((1,)),
        ],
        compiler_params=pltpu.CompilerParams(
            collective_id=0, has_side_effects=True, vmem_limit_bytes=62 * MIB
        ),
        name="forward",
    )(rows, wq, wk, wv, wo, gate, up, down, gains, token_rows, angles, top)


COLUMN_MATRICES = (0, 3)

ORDER = (
    "d", "d", "A", "d", "f1", "p", "f0", "s1", "d", "p", "s0", "d", "p", "d", "d", "p", "d", "d",
    "p", "T", "N", "p", "d", "p", "R", "d", "p", "d", "p", "G", "D", "a", "a", "d", "r", "p", "d",
    "q", "F1", "d", "F0", "d", "p", "d", "S1", "p", "p", "p", "p", "d", "d", "p", "d", "S0", "p",
    "p", "d", "p", "d", "p", "p", "d", "p", "d", "p", "T2", "p",
)


class Collect:
    def __init__(self, place, pieces, depth, gbuf, ybuf, zbuf, ring, came, have, ready, kept, local, ysends,
                 yrecvs, zsends, zrecvs, loads, keeps):
        self.place, self.pieces, self.depth = place, pieces, depth
        columns = [matrix in COLUMN_MATRICES for matrix, _, _, _ in pieces]
        at = [columns[:p].count(columns[p]) for p in range(len(pieces))]
        self.gbuf, self.ybuf, self.zbuf = (
            [bufs[columns[p]].at[at[p]] for p in range(len(pieces))] for bufs in (gbuf, ybuf, zbuf)
        )
        self.ring = ring
        self.came, self.have, self.ready, self.kept = came, have, ready, kept
        self.loads, self.settled = loads, []
        self.made = self.launched = self.summed = 0
        self.flying = []
        self.local, self.over, self.line, self.keep = [], [], [], []
        slot = 0
        for p, (matrix, rows, wide, kind) in enumerate(pieces):
            box = (pl.ds(0, rows), pl.ds(0, wide))
            self.local.append(
                pltpu.make_async_copy(ring.at[(p % 2, slice(None)) + box], self.gbuf[p].at[(slice(None),) + box], local.at[p])
            )
            self.over.append(
                send(
                    self.gbuf[p].at[(1 - place.low,) + box],
                    self.ybuf[p].at[box],
                    ysends,
                    yrecvs,
                    p,
                    place.across(),
                )
            )
            self.keep.append(
                pltpu.make_async_copy(self.gbuf[p].at[(place.low,) + box], have.at[box], loads.at[0])
            )
            if kind == (0, 0):
                self.line.append(None)
                self.settled.append(
                    pltpu.make_async_copy(kept[matrix], self.zbuf[p].at[box], keeps.at[len(self.settled)])
                )
                continue
            self.line.append(
                send(
                    ready.at[(slot % ready.shape[0],) + box],
                    self.zbuf[p].at[box],
                    zsends,
                    zrecvs,
                    p,
                    place.line(*kind),
                )
            )
            slot += 1

    def owner(self, p):
        both = 2 * self.depth
        return pl.ds(pl.multiple_of(self.place.high_at(*self.pieces[p][3]) * both, both), both)

    def make_rows(self, left, right, first):
        p = self.made
        self.launch()
        ring = self.ring.at[p % 2]
        wide = self.pieces[p][2]
        step = 256

        @pl.loop(0, wide // step)
        def _(n):
            lanes = pl.ds(pl.multiple_of(first + n * step, step), step)
            to = pl.ds(pl.multiple_of(n * step, step), step)
            for low in (0, 1):
                rows = left[low * self.depth : (low + 1) * self.depth]
                ring[low, : self.depth, to] = product(rows, right[:, lanes]).astype(BF)

        self.local[p].start()
        self.made = p + 1

    def make_columns(self, left, right):
        p = self.made
        self.launch()
        ring = self.ring.at[p % 2]
        _, rows, wide, _ = self.pieces[p]
        number = left.shape[0] // rows
        pitch = wide // number
        tokens = right.shape[0] * right.shape[1]
        cols = right[:, :, self.owner(p)].reshape(tokens, 2 * self.depth)
        for c in range(number):
            out = product(left[c * rows : (c + 1) * rows], cols).astype(BF)
            for low in (0, 1):
                ring[low, :rows, c * pitch : c * pitch + self.depth] = out[
                    :, low * self.depth : (low + 1) * self.depth
                ]
        self.local[p].start()
        self.made = p + 1

    def launch(self):
        while self.launched < self.made:
            self.local[self.launched].wait()
            self.over[self.launched].start()
            self.launched += 1

    def pump(self, number=1):
        self.launch()
        for _ in range(number):
            p = self.summed
            if p >= self.made:
                return
            matrix, rows, wide, kind = self.pieces[p]
            box = (slice(0, rows), slice(0, wide))
            self.keep[p].start()
            self.over[p].wait_recv()
            came = pltpu.make_async_copy(
                self.ybuf[p].at[pl.ds(0, rows), pl.ds(0, wide)],
                self.came.at[pl.ds(0, rows), pl.ds(0, wide)],
                self.loads.at[2],
            )
            came.start()
            self.keep[p].wait()
            came.wait()
            total = self.came[box].astype(F32) + self.have[box].astype(F32)
            if kind == (0, 0):
                self.kept[matrix][...] = total.astype(BF)
                self.settled[matrix].start()
            else:
                slots = self.ready.shape[0]
                if len(self.flying) >= slots:
                    self.flying[-slots].wait_send()
                self.ready[(len(self.flying) % slots,) + box] = total.astype(BF)
                self.line[p].start()
                self.flying.append(self.line[p])
            self.summed = p + 1

    def drain(self):
        for copy in self.over:
            copy.wait_send()
        for copy in self.flying[-self.ready.shape[0] :]:
            copy.wait_send()
        for copy in self.line:
            if copy is not None:
                copy.wait_recv()
        for copy in self.settled:
            copy.wait()


def backward_kernel(
    count, pieces,
    gffn_in, hidden_in, gate_in, up_in, mid_in, rows_in, full, mixed_in, q_in, k_in, v_in, qh_in, kh_in, inv_in,
    cos_in, sin_in, probs_in, normed_ref, ainv_ref, top_ref, gains_ref, pgain_ref,
    grad_rows, gain_sums,
    gbuf_r, gbuf_c, ybuf_r, ybuf_c, zbuf_r, zbuf_c,
    rows_a, rows_c, hidden, acts, floats, weights, parts, from_core, from_chips, total, resid, turned, ring,
    came, have, ready, kept0, kept1, kept2, kept3, kept4, kept5,
    mixed, q_rot, k_rot, v_low, q_hat, k_hat, inv, cos_ref, sin_ref, probs_ref, datt, dqkv, stats, side_sums, all_sums,
    big_loads, loads, local, ysends, yrecvs, zsends, zrecvs, rsends, rrecvs, r2sends, r2recvs, gsends, grecvs,
    ssends, srecvs, xsends, xrecvs, fsends, frecvs, keeps,
):
    place = Place(count)
    own, width = top_ref.shape
    tokens = 8 * own
    big = tokens // 2
    cols = mixed.shape[0]
    heads = cols // HD
    steps = hidden.shape[0] // cols
    depth = width // count
    others = [(place.index + step) % count for step in range(1, count)]
    tensor_peers = [(0, 1), (1, 0), (1, 1)]

    used = [0]

    def load(src, into):
        copy = pltpu.make_async_copy(src, into, big_loads.at[used[0]])
        used[0] += 1
        copy.start()
        return copy

    def chunk(ref, j):
        return ref.at[:, pl.ds(j * cols, cols)]

    rows_load = load(gffn_in, rows_a)
    hidden_load = load(hidden_in, hidden)
    firsts = [
        [
            load(full.at[4 + 2 * steps + j], chunk(weights, j)),
            load(chunk(gate_in, j), floats.at[2 * (j % 2)]),
            load(chunk(up_in, j), floats.at[2 * (j % 2) + 1]),
        ]
        for j in range(min(2, steps))
    ]
    for j in range(2, steps):
        firsts.append([load(full.at[4 + 2 * steps + j], chunk(weights, j))])
    greet(
        [{"fsdp": other, "tensor": place.tensor} for other in others]
        + [place.peer(p, c, s) for p, c, s in place.group() if c or s]
    )
    kept = [kept0, kept1, kept2, kept3, kept4, kept5]
    collect = Collect(
        place, pieces, depth, (gbuf_r, gbuf_c), (ybuf_r, ybuf_c), (zbuf_r, zbuf_c), ring, came, have, ready, kept, local,
        ysends, yrecvs, zsends, zrecvs, loads, keeps,
    )
    number = len(place.lines()) + 1

    wanted = [(mid_in, number + 2 * k) for k in range(number)] + [
        (rows_in, (4 + turn) * number + k) for turn in range(2) for k in range(number)
    ]
    blocks = []

    def next_block():
        i = len(blocks)
        if i < len(wanted):
            ref, p = wanted[i]
            blocks.append(load(ref.at[collect.owner(p)], turned.at[i % 2]))

    next_block()
    next_block()
    waited = set()

    def once(*copies):
        for copy in copies:
            if id(copy) not in waited:
                waited.add(id(copy))
                copy.wait()

    def make_down():
        once(rows_load, hidden_load)
        collect.make_columns(hidden, rows_a)

    def make_rows(i, right, first, last):
        once(blocks[i])
        collect.make_rows(turned.at[i % 2], right, first)
        if last:
            next_block()

    makes = [make_down] * number
    for k in range(number):
        makes.append(functools.partial(make_rows, k, acts, 0, False))
        makes.append(functools.partial(make_rows, k, acts, steps * cols, True))
    def make_out():
        once(*late["rest"])
        collect.make_columns(mixed, rows_c)

    makes += [make_out] * number
    for turn, first in ((1, 2 * cols), (2, 0)):
        for k in range(number):
            makes.append(functools.partial(make_rows, turn * number + k, dqkv, first, True))

    late = {}

    def gate_and_up():
        once(rows_load)
        for j in range(steps):
            once(*firsts[j])
            at = 2 * (j % 2)

            @pl.loop(0, 4)
            def _(i):
                m = pl.ds(pl.multiple_of(i * 2 * own, 2 * own), 2 * own)
                left = rows_a[pl.ds(i * 2, 2)].reshape(2 * own, width)
                grad = product(left, weights[:, j * cols : (j + 1) * cols])
                acts[m, 2 * j * cols : (2 * j + 1) * cols] = (grad * floats[at, m]).astype(BF)
                acts[m, (2 * j + 1) * cols : (2 * j + 2) * cols] = (grad * floats[at + 1, m]).astype(BF)

            if j + 2 < steps:
                firsts[j + 2] += [
                    load(chunk(gate_in, j + 2), floats.at[at]),
                    load(chunk(up_in, j + 2), floats.at[at + 1]),
                ]
        late["ffn"] = [load(full.at[4 + c], chunk(weights, c)) for c in range(2 * steps)]
        late["rest"] = [
            load(src, into)
            for src, into in (
                (mixed_in, mixed), (q_in, q_rot), (k_in, k_rot), (v_in, v_low), (qh_in, q_hat), (kh_in, k_hat),
                (inv_in, inv), (cos_in, cos_ref), (sin_in, sin_ref), (probs_in, probs_ref),
            )
        ]

    tile = tiles(acts, weights, parts, pl.ds(0, acts.shape[1]))
    scatter = Scatter(place, tile, parts, from_core, from_chips, total, rsends, rrecvs, via=True)
    tile = tiles(dqkv, weights, parts, pl.ds(0, 3 * cols))
    again = Scatter(place, tile, parts, from_core, from_chips, total, r2sends, r2recvs, via=True)
    gather = Gather(place, rows_c, gsends, grecvs)
    wide = width // gains_ref.shape[1]
    lanes_per = gains_ref.shape[1]
    cut = lambda row: [row[:, r * lanes_per : (r + 1) * lanes_per] for r in range(wide)]
    side_copies, inner_copies, all_copies = [], [], []

    def first(pair):
        once(*late["ffn"])
        scatter.first(pair)

    def second(pair):
        scatter.second(pair)
        if not pair:
            scatter.relay()
            late["att"] = [load(full.at[c], chunk(weights, c)) for c in range(4)]

    def norm():
        normed = normed_ref[...]
        gain = jnp.concatenate([gains_ref[r : r + 1] for r in range(wide)], axis=1)
        grad = top_ref[...].astype(F32) + total[...]
        resid[...] = grad
        part_gain = jnp.sum(grad * normed, axis=0, keepdims=True)
        scaled = grad * gain
        inner = jnp.mean(scaled * normed, axis=1, keepdims=True)
        rows_c[place.slot()] = (ainv_ref[:, :1] * (scaled - normed * inner)).astype(BF)
        gather.start()
        side_sums[place.tensor] = jnp.concatenate(cut(part_gain) + cut(pgain_ref[0:1]), axis=0)
        for i, (c, s) in enumerate(tensor_peers):
            copy = send(
                side_sums.at[place.tensor], side_sums.at[place.tensor], xsends, xrecvs, i, place.peer(0, c, s)
            )
            copy.start()
            side_copies.append(copy)

    def out_back():
        once(*late["att"], *late["rest"])

        @pl.loop(0, 4)
        def _(i):
            m = pl.ds(pl.multiple_of(i * 2 * own, 2 * own), 2 * own)
            left = rows_c[pl.ds(i * 2, 2)].reshape(2 * own, width)
            datt[m] = product(left, weights[:, 3 * cols : 4 * cols]).astype(BF)

    scale = HD ** (-0.5)
    quarter = big // 2

    def attend(block, h):
        lanes = pl.ds(pl.multiple_of(h * HD, HD), HD)
        k_at = pl.ds(pl.multiple_of(block * big, big), big)
        keys = k_rot[k_at, lanes]
        values = v_low[k_at, lanes]
        for half in range(2):
            q_at = pl.ds(pl.multiple_of(block * big + half * quarter, quarter), quarter)
            queries = q_rot[q_at, lanes]
            grads = datt[q_at, lanes]
            low = probs_ref[block * heads + h, half * quarter : (half + 1) * quarter]
            probs = low.astype(F32)
            dprobs = product_last(grads, values)
            inner = jnp.sum(probs * dprobs, axis=1, keepdims=True)
            dscores = (probs * (dprobs - inner)).astype(BF)
            floats[0, q_at, lanes] = product(dscores, keys) * scale
            dkeys = product_first(dscores, queries) * scale
            dvalues = product_first(low, grads)
            if half:
                floats[1, k_at, lanes] += dkeys
                floats[2, k_at, lanes] += dvalues
            else:
                floats[1, k_at, lanes] = dkeys
                floats[2, k_at, lanes] = dvalues

    attended = [0]

    def attention():
        pl.loop(0, heads)(functools.partial(attend, attended[0]))
        m = pl.ds(attended[0] * big, big)
        dqkv[m, 2 * cols :] = floats[2, m].astype(BF)
        attended[0] += 1

    def rotate_back():
        gain_at = pl.ds(pl.multiple_of(place.pair * cols, cols), cols)
        norm_gains = [gains_ref[2 * wide + which : 2 * wide + which + 1, gain_at] for which in (0, 1)]
        gain_parts, inners = [], []
        for which, hat in ((0, q_hat), (1, k_hat)):
            pieces_of = []
            for h in range(heads):
                lanes = slice(h * HD, (h + 1) * HD)
                value = floats[which, :, lanes]
                value = value * cos_ref[...] - pltpu.roll(value, HD // 2, 1) * sin_ref[...]
                weighted = value * hat[:, lanes]
                gain_parts.append(jnp.sum(weighted, axis=0, keepdims=True))
                part = norm_gains[which][:, lanes]
                pieces_of.append(jnp.sum(weighted * part, axis=1, keepdims=True))
                floats[which, :, lanes] = value * part
            inners.append(sum(pieces_of[1:], pieces_of[0]))
        inner_copies.extend(exchange_sums(place, stats, inners, ssends, srecvs))
        for copy in side_copies:
            copy.wait_recv()
        side = side_sums[0]
        for t in range(1, side_sums.shape[0]):
            side = side + side_sums[t]
        gain_rows = [jnp.concatenate(gain_parts[w * heads : (w + 1) * heads], axis=1) for w in (0, 1)]
        upper = place.pair == 1
        gain_rows = [
            jnp.concatenate([jnp.where(upper, 0.0, row), jnp.where(upper, row, 0.0)], axis=1) for row in gain_rows
        ]
        spare = jnp.zeros((all_sums.shape[1] - 2 * wide - 2, lanes_per), F32)
        all_sums[place.index] = jnp.concatenate([side] + gain_rows + [spare], axis=0)
        for i, other in enumerate(others):
            copy = send(
                all_sums.at[place.index], all_sums.at[place.index], fsends, frecvs, i,
                {"fsdp": other, "tensor": place.tensor},
            )
            copy.start()
            all_copies.append(copy)

    def query_key():
        sums = finish_sums(stats, inner_copies) / width
        for which, hat in ((0, q_hat), (1, k_hat)):
            lanes_inner = over_lanes(sums[which : which + 1])
            for h in range(heads):
                lanes = slice(h * HD, (h + 1) * HD)
                value = inv[which] * (floats[which, :, lanes] - hat[:, lanes] * lanes_inner)
                dqkv[:, which * cols + h * HD : which * cols + (h + 1) * HD] = value.astype(BF)

    def first_again(pair):
        if pair:
            scatter.drain()
        again.first(pair)

    def second_again(pair):
        again.second(pair)
        if not pair:
            again.relay()

    grad_copies = []

    def third_again():
        again.third()
        total[...] += resid[...]
        grad_copies.append(load(total, grad_rows))

    actions = {
        "A": gate_and_up,
        "f1": lambda: first(1),
        "f0": lambda: first(0),
        "s1": lambda: second(1),
        "s0": lambda: second(0),
        "T": scatter.third,
        "N": norm,
        "R": gather.relay,
        "G": gather.finish,
        "D": out_back,
        "a": attention,
        "r": rotate_back,
        "q": query_key,
        "F1": lambda: first_again(1),
        "F0": lambda: first_again(0),
        "S1": lambda: second_again(1),
        "S0": lambda: second_again(0),
        "T2": third_again,
    }
    each = number // 4
    for name in ORDER:
        if name == "d":
            for _ in range(each):
                makes.pop(0)()
        elif name == "p":
            collect.pump(each)
        else:
            actions[name]()
    for copy in all_copies:
        copy.wait_recv()
    sums = all_sums[0]
    for f in range(1, count):
        sums = sums + all_sums[f]
    gain_sums[...] = sums
    for copy in grad_copies:
        copy.wait()
    collect.drain()
    again.drain()
    gather.drain()
    for copy in inner_copies + side_copies + all_copies:
        copy.wait_send()


def list_pieces(count, depth, cols, half):
    kinds = line_kinds(count) + [(0, 0)]
    pitch = max(depth, 128)
    sizes = [
        (cols, half // cols * pitch), (depth, half), (depth, half), (cols, pitch), (depth, cols), (depth, 2 * cols),
    ]
    order = [[0], [1, 2], [3], [4], [5]]
    return sizes, [(m,) + sizes[m] + (kind,) for group in order for kind in kinds for m in group]


def settle_kernel(
    pieces, zbuf_r, zbuf_c, grad_in, out_in,
    out_q, out_k, out_v, out_o, out_gate, out_up, out_down, grad_out, out_out,
    boxes_r, boxes_c, grad_held, out_held, stage0, stage1, stage2, stage3, stage4, stage5, loads, stores, copies,
):
    stages = [stage0, stage1, stage2, stage3, stage4, stage5]
    whole = []
    for i, (src, held_here, dst) in enumerate(((grad_in, grad_held, grad_out), (out_in, out_held, out_out))):
        into = pltpu.make_async_copy(src, held_here, copies.at[i])
        into.start()
        whole.append((into, pltpu.make_async_copy(held_here, dst, copies.at[2 + i])))
    pair = lax.axis_index("fsdp") // 2 % 2
    held, count = [], [0, 0]
    for p, (matrix, _, _, _) in enumerate(pieces):
        column = matrix in COLUMN_MATRICES
        at = count[column]
        count[column] += 1
        zbuf, boxes = (zbuf_c, boxes_c) if column else (zbuf_r, boxes_r)
        _, rows, wide, _ = pieces[p]
        box = (pl.ds(0, rows), pl.ds(0, wide))
        copy = pltpu.make_async_copy(zbuf.at[(at,) + box], boxes.at[(at,) + box], loads.at[p])
        copy.start()
        held.append((copy, boxes, at))
    for into, back in whole:
        into.wait()
        back.start()
    cols = out_q.shape[1] // 2
    steps = out_gate.shape[1] // 2 // cols
    both = [(ref, j * cols) for j in range(steps) for ref in (out_gate, out_up)]
    groups = [
        [(out_down, None)] * steps,
        both[:steps],
        both[steps:],
        [(out_o, None)],
        [(out_v, 0)],
        [(out_q, 0), (out_k, 0)],
    ]
    sent = []
    for matrix, targets in enumerate(groups):
        for p, (m, _, _, _) in enumerate(pieces):
            if m == matrix:
                held[p][0].wait()
        stage = stages[matrix]
        rows, wide = stage.shape[1:]
        step = min(rows, 64)

        @pl.loop(0, rows // step)
        def _(i):
            at = pl.ds(pl.multiple_of(i * step, step), step)
            sums = [None, None]
            for p, (m, _, _, kind) in enumerate(pieces):
                if m != matrix:
                    continue
                _, boxes, index = held[p]
                part = boxes[index, at, :wide].astype(F32)
                which = kind[1]
                sums[which] = part if sums[which] is None else sums[which] + part
            stage[0, at] = sums[0]
            stage[1, at] = sums[1]

        pitch = wide // len(targets)
        for r in (0, 1):
            half = flip(pair, r)
            for c, (ref, at) in enumerate(targets):
                src = stage.at[r, :, pl.ds(c * pitch, pitch)]
                if at is None:
                    start = half * (ref.shape[0] // 2) + c * rows
                    dst = ref.at[pl.ds(pl.multiple_of(start, rows), rows)]
                else:
                    start = half * (ref.shape[1] // 2) + at
                    dst = ref.at[:, pl.ds(pl.multiple_of(start, pitch), pitch)]
                copy = pltpu.make_async_copy(src, dst, stores.at[len(sent)])
                copy.start()
                sent.append(copy)
    for copy in sent + [back for _, back in whole]:
        copy.wait()


def run_settle(count, cols, half, zbuf_r, zbuf_c, grad, output):
    width = grad.shape[1]
    depth = width // count
    sizes, pieces = list_pieces(count, depth, cols, half)
    pitch = max(depth, 128)
    shape = jax.ShapeDtypeStruct
    small = shape((depth, 2 * cols), F32)
    large = shape((depth, 2 * half), F32)
    outs = (
        small, small, small, shape((2 * cols, pitch), F32),
        large, large, shape((2 * half, pitch), F32),
        shape(grad.shape, grad.dtype), shape(output.shape, output.dtype),
    )
    return pl.pallas_call(
        functools.partial(settle_kernel, pieces),
        out_shape=outs,
        in_specs=[ANY] * 4,
        out_specs=[ANY] * len(outs),
        scratch_shapes=[
            pltpu.VMEM(zbuf_r.shape, BF),
            pltpu.VMEM(zbuf_c.shape, BF),
            pltpu.VMEM(grad.shape, grad.dtype),
            pltpu.VMEM(output.shape, output.dtype),
            *[pltpu.VMEM((2,) + size, F32) for size in sizes],
            DMA((len(pieces),)), DMA((64,)), DMA((4,)),
        ],
        compiler_params=pltpu.CompilerParams(vmem_limit_bytes=62 * MIB),
        name="settle",
    )(zbuf_r, zbuf_c, grad, output)


def run_backward(
    count, gffn, hidden, gate, up, mid, rows, full, mixed, q_rot, k_rot, v_low, q_hat, k_hat, inv, cosine, sine, probs,
    normed, ainv, top, gains, part_gain,
):
    own, width = top.shape
    tokens = 8 * own
    cols = mixed.shape[0]
    half = hidden.shape[0]
    depth = width // count
    steps = half // cols
    pitch = max(depth, 128)
    kinds = line_kinds(count) + [(0, 0)]
    sizes, pieces = list_pieces(count, depth, cols, half)
    number = len(pieces)
    kinds_of = ((4 * len(kinds), sizes[1]), (2 * len(kinds), sizes[0]))
    box = (max(depth, cols), half)
    shape = jax.ShapeDtypeStruct
    outs = (
        shape((own, width), F32),
        shape(gains.shape, F32),
        *[shape((n,) + lead + size, BF) for lead in ((2,), (), ()) for n, size in kinds_of],
    )
    like = lambda array: pltpu.VMEM(array.shape, array.dtype)
    return pl.pallas_call(
        functools.partial(backward_kernel, count, pieces),
        out_shape=outs,
        in_specs=[ANY] * 17 + [VMEM] * 5,
        out_specs=[ANY, VMEM] + [ANY] * 6,
        scratch_shapes=[
            like(gffn), like(gffn), like(hidden),
            pltpu.VMEM((tokens, 2 * half), BF),
            pltpu.VMEM((4, tokens, cols), F32),
            pltpu.VMEM((width, 2 * half), BF),
            pltpu.VMEM((8, own, width), BF),
            pltpu.VMEM((4, own, width), BF),
            pltpu.VMEM((3, own, width), BF),
            pltpu.VMEM((own, width), F32),
            pltpu.VMEM((own, width), F32),
            pltpu.VMEM((2, 2 * depth, tokens), BF),
            pltpu.VMEM((2, 2) + box, BF),
            pltpu.VMEM(box, BF),
            pltpu.VMEM(box, BF),
            pltpu.VMEM((6,) + box, BF),
            *[pltpu.VMEM(size, BF) for size in sizes],
            like(mixed), like(q_rot), like(k_rot), like(v_low), like(q_hat), like(k_hat), like(inv),
            like(cosine), like(sine), like(probs),
            pltpu.VMEM((tokens, cols), BF),
            pltpu.VMEM((tokens, 3 * cols), BF),
            pltpu.VMEM((8, 8, tokens), F32),
            pltpu.VMEM((4, 2 * width // gains.shape[1], gains.shape[1]), F32),
            pltpu.VMEM((count,) + gains.shape, F32),
            DMA((64 + 3 * len(kinds),)), DMA((3,)), DMA((number,)),
            DMA((number,)), DMA((number,)),
            DMA((number,)), DMA((number,)),
            DMA((7,)), DMA((7,)),
            DMA((7,)), DMA((7,)),
            DMA((9,)), DMA((9,)),
            DMA((7,)), DMA((7,)),
            DMA((3,)), DMA((3,)),
            DMA((count - 1,)), DMA((count - 1,)),
            DMA((6,)),
        ],
        compiler_params=pltpu.CompilerParams(
            collective_id=1, has_side_effects=True, vmem_limit_bytes=63 * MIB
        ),
        name="backward",
    )(
        gffn, hidden, gate, up, mid, rows, full, mixed, q_rot, k_rot, v_low, q_hat, k_hat, inv, cosine, sine, probs,
        normed, ainv, top, gains, part_gain,
    )


def local(
    inputs,
    seg_ids,
    positions,
    w_query,
    w_key,
    w_value,
    w_out,
    query_gain,
    key_gain,
    attn_gain,
    w_gate,
    w_up,
    w_down,
    ffn_gain,
    out_grad,
    count,
    tensor,
):
    index = lax.axis_index("fsdp")
    own_rows, width = inputs.shape
    group_rows = seg_ids.shape[0]
    depth = width // count

    heads_here, part = query_gain.shape
    heads_half = heads_here // 2
    cols = heads_half * HD
    sizes = heads_here * part

    def placed(values, copies):
        size = values.shape[-1]
        here = jnp.arange(size * count, dtype=jnp.int32) // size == index
        return jnp.where(here, jnp.tile(values, copies), 0).reshape(-1, heads_here * HD)

    packed = jnp.concatenate(
        [
            placed(attn_gain, count),
            placed(ffn_gain, count),
            placed(jnp.concatenate([query_gain, key_gain]), (1, count)),
        ]
    )
    packed = jnp.pad(packed, ((0, -packed.shape[0] % 16), (0, 0)))

    token_rows = jnp.pad(jnp.stack([positions, seg_ids]).astype(F32), ((0, 6), (0, 0)))
    freq = np.float32(ROPE_THETA) ** (-(np.arange(HD // 2, dtype=np.float32) * 2) / np.float32(HD))
    angles = np.zeros((8, HD), np.float32)
    angles[0] = np.concatenate([freq, freq])
    angles[1] = np.concatenate([-np.ones(HD // 2), np.ones(HD // 2)])
    turned = depth % 128 != 0

    (
        full, gains, query_rot, key_rot, value_low, query_hat, key_hat, invs, attn_normed, attn_inv, gate_raw, up_raw,
        output, partial_ffn_gain, probs, cosine, sine, rows_grad_ffn, mixed_low, hidden_low, all_rows, rows_mid,
    ) = run_forward(
        count, inputs, w_query, w_key, w_value, w_out.T if turned else w_out, w_gate, w_up,
        w_down.T if turned else w_down, packed, token_rows, angles, out_grad,
    )
    wide = width // gains.shape[1]
    (
        grad_rows, gain_sums, _, _, _, _, zbuf_r, zbuf_c,
    ) = run_backward(
        count, rows_grad_ffn, hidden_low, gate_raw, up_raw, rows_mid, all_rows, full, mixed_low, query_rot,
        key_rot, value_low, query_hat, key_hat, invs, cosine, sine, probs, attn_normed, attn_inv,
        out_grad, gains, partial_ffn_gain,
    )

    (
        sum_query, sum_key, sum_value, sum_out, sum_gate, sum_up, sum_down, grad_inputs, output,
    ) = run_settle(count, cols, hidden_low.shape[0], zbuf_r, zbuf_c, grad_rows, output)

    def own_gain(row):
        return lax.dynamic_slice_in_dim(gain_sums[row * wide : (row + 1) * wide].reshape(-1), index * depth, depth)

    def own_head_gain(row):
        values = gain_sums[2 * wide + row].reshape(heads_here, HD)
        return lax.dynamic_slice_in_dim(values, index * part, part, 1)

    return (
        output,
        grad_inputs,
        sum_query,
        sum_key,
        sum_value,
        sum_out[:, :depth],
        own_head_gain(0),
        own_head_gain(1),
        own_gain(0),
        sum_gate,
        sum_up,
        sum_down[:, :depth],
        own_gain(1),
    )


def solution(mesh):
    count = mesh.shape["fsdp"]
    tensor = mesh.shape["tensor"]
    tokens = P(("fsdp", "tensor"), None)
    rows = P("fsdp", "tensor")
    columns = P("tensor", "fsdp")
    line = P("fsdp")

    def body(*arrays):
        return local(*arrays, count=count, tensor=tensor)

    return jax.shard_map(
        body,
        mesh=mesh,
        in_specs=(
            tokens, line, line, rows, rows, rows, columns, columns, columns, line,
            rows, rows, columns, line, tokens,
        ),
        out_specs=(
            tokens, tokens, rows, rows, rows, columns, columns, columns, line,
            rows, rows, columns, line,
        ),
        check_vma=False,
    )
```

```python
import functools

import jax
import jax.numpy as jnp
import numpy as np
from jax import lax
from jax.experimental import pallas as pl
from jax.experimental.pallas import tpu as pltpu
from jax.sharding import PartitionSpec as P

HD = 128
NORM_EPS = 1e-06
ROPE_THETA = 500000.0
BF = jnp.bfloat16
F32 = jnp.float32
MIB = 1 << 20


class Place:
    def __init__(self, count):
        self.count = count
        self.outers = count // 4
        self.index = lax.axis_index("fsdp")
        self.tensor = lax.axis_index("tensor")
        self.low = self.index % 2
        self.high = self.index // 2
        self.pair = self.high % 2
        self.outer = self.high // 2
        self.core = self.tensor % 2
        self.side = self.tensor // 2

    def device(self, outer, pair, low, core, side):
        return {"fsdp": (outer * 2 + pair) * 2 + low, "tensor": side * 2 + core}

    def peer(self, pair=0, core=0, side=0):
        return self.device(
            self.outer, flip(self.pair, pair), self.low, flip(self.core, core), flip(self.side, side)
        )

    def slot(self, pair=0, core=0, side=0):
        return flip(self.pair, pair) * 4 + flip(self.core, core) * 2 + flip(self.side, side)

    def line(self, step, pair):
        outer = (self.outer + step) % self.outers
        return self.device(outer, flip(self.pair, pair), self.low, self.core, self.side)

    def high_at(self, step, pair):
        return ((self.outer + step + self.outers) % self.outers) * 2 + flip(self.pair, pair)

    def across(self):
        return self.device(self.outer, self.pair, 1 - self.low, self.core, self.side)

    def lines(self):
        return line_kinds(self.count)

    def group(self):
        return [(p, c, s) for p in (0, 1) for c in (0, 1) for s in (0, 1) if p or c or s]


def line_kinds(count):
    return [(step, pair) for step in reversed(range(count // 4)) for pair in (0, 1) if step or pair]


def flip(bit, yes):
    return 1 - bit if yes else bit


def greet(devices):
    barrier = pltpu.get_barrier_semaphore()
    for device in devices:
        pl.semaphore_signal(barrier, inc=1, device_id=device, device_id_type=pl.DeviceIdType.MESH)
    pl.semaphore_wait(barrier, len(devices))


def send(src, dst, sends, recvs, slot, device):
    return pltpu.make_async_remote_copy(
        src_ref=src,
        dst_ref=dst,
        send_sem=sends.at[slot],
        recv_sem=recvs.at[slot],
        device_id=device,
        device_id_type=pl.DeviceIdType.MESH,
    )


def product(left, right):
    return lax.dot_general(left, right, (((1,), (0,)), ((), ())), preferred_element_type=F32)


def product_last(left, right):
    return lax.dot_general(left, right, (((1,), (1,)), ((), ())), preferred_element_type=F32)


def product_first(left, right):
    return lax.dot_general(left, right, (((0,), (0,)), ((), ())), preferred_element_type=F32)


class Gather:
    slots = 9

    def __init__(self, place, rows, sends, recvs, split=False):
        half = rows.shape[1] // 2

        def go(slot, device, part=None, **kw):
            ref = rows.at[place.slot(**kw)]
            if part is not None:
                ref = rows.at[place.slot(**kw), pl.ds(part * half, half)]
            return send(ref, ref, sends, recvs, slot, place.peer(**device))

        self.to_pair = go(0, dict(pair=1))
        self.to_side = go(1, dict(side=1))
        self.to_core = go(2, dict(core=1))
        self.pair_to_core = go(5, dict(core=1), pair=1)
        self.side_to_core = go(6, dict(core=1), side=1)
        if split:
            self.relays = [go(3, dict(side=1), 0, pair=1), go(4, dict(pair=1), 1, side=1)]
            self.last = [go(7, dict(core=1), 0, pair=1, side=1), go(8, dict(core=1), 1, pair=1, side=1)]
        else:
            self.relays = [go(3, dict(side=1), pair=1)]
            self.last = [go(7, dict(core=1), pair=1, side=1)]

    def start(self):
        self.to_pair.start()
        self.to_side.start()
        self.to_core.start()

    def relay(self):
        self.to_pair.wait_recv()
        self.relays[0].start()
        self.pair_to_core.start()
        self.to_side.wait_recv()
        for copy in self.relays[1:]:
            copy.start()
        self.side_to_core.start()

    def finish(self):
        for relay, copy in zip(self.relays, self.last):
            relay.wait_recv()
            copy.start()
        for copy in [self.to_core, self.pair_to_core, self.side_to_core] + self.last:
            copy.wait_recv()

    def drain(self):
        for copy in [self.to_pair, self.to_side, self.to_core, self.pair_to_core, self.side_to_core]:
            copy.wait_send()
        for copy in self.relays + self.last:
            copy.wait_send()


class Scatter:
    order = [(1, 1), (1, 0), (0, 1), (0, 0)]

    def __init__(self, place, tile, parts, from_core, from_chips, total, sends, recvs, via=False):
        self.place, self.tile, self.parts = place, tile, parts
        self.from_core, self.from_chips, self.total, self.via = from_core, from_chips, total, via
        self.to_core = [
            send(
                parts.at[place.slot(pair=pair, core=1, side=side)],
                from_core.at[slot],
                sends,
                recvs,
                slot,
                place.peer(core=1),
            )
            for slot, (pair, side) in enumerate(self.order)
        ]
        self.to_chips = [
            send(
                parts.at[place.slot(pair=pair, side=side)],
                from_chips.at[slot],
                sends,
                recvs,
                4 + slot,
                place.peer(pair=pair if slot or not via else 0, side=side),
            )
            for slot, (pair, side) in enumerate(self.order[:3])
        ]

    def first(self, pair):
        place = self.place
        self.tile(flip(place.pair, pair), 1 - place.core)
        for slot, (p, side) in enumerate(self.order):
            if p == pair:
                self.to_core[slot].start()

    def both(self, slot):
        pair, side = self.order[slot]
        mine = self.place.slot(pair=pair, side=side)
        return mine, self.parts[mine].astype(F32) + self.from_core[slot].astype(F32)

    def second(self, pair):
        self.tile(flip(self.place.pair, pair), self.place.core)
        for slot, (p, side) in enumerate(self.order):
            if p != pair:
                continue
            self.to_core[slot].wait_recv()
            if self.via and slot == 1:
                continue
            mine, both = self.both(slot)
            if slot < 3:
                self.parts[mine] = both.astype(BF)
                self.to_chips[slot].start()
            else:
                self.total[...] = both

    def relay(self):
        if self.via:
            self.to_chips[0].wait_recv()
            mine, both = self.both(1)
            self.parts[mine] = (both + self.from_chips[0].astype(F32)).astype(BF)
            self.to_chips[1].start()

    def third(self):
        for slot, copy in enumerate(self.to_chips):
            if slot or not self.via:
                copy.wait_recv()
                self.total[...] += self.from_chips[slot].astype(F32)

    def drain(self):
        for copy in self.to_core + self.to_chips:
            copy.wait_send()


def tiles(left_ref, right, parts, lanes):
    own, width = parts.shape[1:]

    def tile(pair, core):
        first = pair * 4 + core * 2
        m = pl.ds(pl.multiple_of(first * own, 2 * own), 2 * own)

        @pl.loop(0, width // 512)
        def _(n):
            at = pl.ds(pl.multiple_of(n * 512, 512), 512)
            out = product_last(left_ref[m, :], right[at, lanes]).astype(BF)
            parts[first, :, at] = out[:own]
            parts[first + 1, :, at] = out[own:]

    return tile


def exchange_sums(place, stats, columns, sends, recvs):
    tokens = stats.shape[2]
    mine = place.slot()
    rows = [jnp.transpose(jnp.broadcast_to(column, (tokens, 128)))[0:1] for column in columns]
    stats[mine] = jnp.concatenate(rows + [jnp.zeros((6, tokens), F32)], axis=0)
    copies = []
    for i, (p, c, s) in enumerate(place.group()):
        copy = send(stats.at[mine], stats.at[mine], sends, recvs, i, place.peer(p, c, s))
        copy.start()
        copies.append(copy)
    return copies


def finish_sums(stats, copies):
    for copy in copies:
        copy.wait_recv()
    sums = stats[0]
    for g in range(1, 8):
        sums = sums + stats[g]
    return sums


def over_lanes(row):
    return jnp.transpose(jnp.broadcast_to(row, (128, row.shape[1])))


class Stream:
    def __init__(self, place, sources, full, sends, recvs, held, local):
        self.place = place
        self.kinds = sorted(place.lines())
        self.lines, self.over, self.hold, self.keep = [], [], [], []
        self.next = self.begun = self.begun_over = 0
        self.ahead, self.over_ahead = 1, 8
        depth = full.shape[1] // place.count
        per = place.count - 1
        for i, source in enumerate(sources):
            def rows(high, low, i=i):
                at = (high * 2 + low) * depth
                return full.at[i, pl.ds(pl.multiple_of(at, depth), depth)]

            own = rows(place.high, place.low)
            first = i * per
            self.lines.append(
                [
                    send(source(flip(place.pair, pair)), own, sends, recvs, first + k, place.line(step, pair))
                    for k, (step, pair) in enumerate(self.kinds)
                ]
            )
            first += len(self.kinds)
            over = [send(source(place.pair), own, sends, recvs, first, place.across())]
            for k, (step, pair) in enumerate(self.kinds):
                block = rows(place.high_at(-step, pair), place.low)
                over.append(send(block, block, sends, recvs, first + 1 + k, place.across()))
            self.over.append(over)
            self.hold.append(pltpu.make_async_copy(source(place.pair), held.at[i], local.at[0, i]))
            self.keep.append(pltpu.make_async_copy(held.at[i], own, local.at[1, i]))

    def place_own(self):
        for copy in self.hold:
            copy.start()
        for hold, keep in zip(self.hold, self.keep):
            hold.wait()
            keep.start()

    def fill(self):
        while self.begun < min(self.next // len(self.kinds) + self.ahead, len(self.lines)):
            for copy in self.lines[self.begun]:
                copy.start()
            self.begun += 1
        while self.begun_over < min(self.next // len(self.kinds) + self.over_ahead, len(self.lines)):
            self.over[self.begun_over][0].start()
            self.begun_over += 1

    def pump(self, number=1):
        per = len(self.kinds)
        for _ in range(number):
            i, k = divmod(self.next, per)
            if i >= len(self.lines):
                return
            self.lines[i][k].wait_recv()
            self.over[i][k + 1].start()
            self.next += 1
            if self.next % per == 0:
                self.fill()

    def arrive(self, i):
        self.pump(max(0, (i + 1) * len(self.kinds) - self.next))
        for copy in self.over[i]:
            copy.wait_recv()
        self.keep[i].wait()

    def drain(self):
        for copies in self.lines + self.over:
            for copy in copies:
                copy.wait_send()


ANY = pl.BlockSpec(memory_space=pl.ANY)
VMEM = pl.BlockSpec(memory_space=pltpu.VMEM)
DMA = pltpu.SemaphoreType.DMA


FORWARD_ORDER = (
    "k", "k", "k", "k", "k", "k", "xr", "k", "w2", "k", "xf", "t", "k", "k", "t", "k", "t", "q0",
    "k", "k", "q1", "q2", "s", "k", "k", "sf", "rope", "k", "k", "k", "k", "a", "a", "k", "k", "k",
    "k", "t", "f", "s1", "k", "k", "k", "k", "k", "s0", "rl", "k", "T", "k", "N", "k", "k", "R",
    "k", "k", "k", "k", "k", "G", "t", "g0", "k", "k", "k", "k", "g1", "t", "k", "k", "w2", "g2",
    "k", "k", "k", "t", "g3", "k", "t", "k", "t", "t",
)


def forward_kernel(
    count,
    rows_ref, q_ref, k_ref, v_ref, o_ref, gate_ref, up_ref, down_ref, gains_ref, tokens_ref, angles_ref, top_ref,
    full, gains_out, q_rot_out, k_rot_out, v_low_out, q_hat_out, k_hat_out, inv_out,
    normed_out, ainv_out, gate_out, up_out, output, part_out, probs_out, cos_out, sin_out, grad_out, mixed_turned, hidden_turned,
    rows_turned, mid_turned,
    all_rows, all_gains, gains, own_rows, att_w, ffn_w, raw, q_rot, k_rot, v_low, q_hat, k_hat, inv_ref,
    normed_ref, ainv_ref, gate_act, up_act, result, part_gain, probs_ref, cos_ref, sin_ref, mixed_t,
    bias_ref, token_rows, o_turned, down_turned, held,
    mixed, mid, hidden, turning, resid_ref, stats, parts, from_core, from_chips, total,
    wsends, wrecvs, keeps, loads, flushes, xsends, xrecvs, nsends, nrecvs, ssends, srecvs,
    rsends, rrecvs, gsends, grecvs, r2sends, r2recvs, g2sends, g2recvs, turn_sems, tsends, trecvs,
):
    place = Place(count)
    own, width = rows_ref.shape
    tokens = 8 * own
    big = tokens // 2
    cols = q_ref.shape[1] // 2
    heads = cols // HD
    mine = place.slot()
    others = [(place.index + step) % count for step in range(1, count)]

    first_copies = [
        pltpu.make_async_copy(rows_ref, all_rows.at[mine], loads.at[0]),
        pltpu.make_async_copy(gains_ref, all_gains.at[place.index], loads.at[1]),
        pltpu.make_async_copy(rows_ref, own_rows, loads.at[2]),
    ]
    for copy in first_copies:
        copy.start()
    turn_here = o_turned.shape[0] % 128 == 0
    if turn_here:
        narrow = [
            pltpu.make_async_copy(o_ref, ffn_w.at[pl.ds(0, o_ref.shape[0]), pl.ds(cols, cols)], loads.at[3]),
            pltpu.make_async_copy(down_ref, ffn_w.at[pl.ds(0, down_ref.shape[0]), pl.ds(0, cols)], loads.at[4]),
        ]
        for copy in narrow:
            copy.start()
    blocks = [side * 2 + core for core in (0, 1) for side in (0, 1)]
    token_rows[place.pair] = jnp.concatenate(
        [tokens_ref[:, block * own : (block + 1) * own] for block in blocks], axis=1
    )
    greet(
        [{"fsdp": other, "tensor": place.tensor} for other in others]
        + [place.peer(p, c, s) for p, c, s in place.group() if c or s]
    )
    token_copy = send(
        token_rows.at[place.pair], token_rows.at[place.pair], tsends, trecvs, 0, place.peer(pair=1)
    )
    token_copy.start()

    def pieces(ref):
        half = ref.shape[1] // 2

        def source(j):
            return lambda h: ref.at[:, pl.ds(pl.multiple_of(h * half + j * cols, cols), cols)]

        return [source(j) for j in range(half // cols)]

    o_source, down_source = (o_turned, down_turned) if turn_here else (o_ref, down_ref)
    gate_pieces, up_pieces = pieces(gate_ref), pieces(up_ref)
    sources = [pieces(ref)[0] for ref in (q_ref, k_ref, v_ref, o_source)]
    for pair in zip(gate_pieces, up_pieces):
        sources.extend(pair)
    sources.extend(pieces(down_source))
    steps = len(gate_pieces)
    stream = Stream(place, sources, full, wsends, wrecvs, held, keeps)
    rows_gather = Gather(place, all_rows, xsends, xrecvs)
    first_copies[0].wait()
    rows_gather.start()
    if turn_here:
        narrow[0].wait()
        o_turned[...] = jnp.transpose(ffn_w[: o_ref.shape[0], cols : 2 * cols])
        narrow[1].wait()
        for block in range(down_ref.shape[0] // 512):
            at = slice(block * 512, (block + 1) * 512)
            down_turned[:, at] = jnp.transpose(ffn_w[at, :cols])
    stream.fill()
    stream.place_own()
    first_copies[1].wait()
    gain_copies = []
    for i, other in enumerate(others):
        copy = send(
            all_gains.at[place.index],
            all_gains.at[place.index],
            nsends,
            nrecvs,
            i,
            {"fsdp": other, "tensor": place.tensor},
        )
        copy.start()
        gain_copies.append(copy)

    flushed = []

    def flush(src, dst):
        copy = pltpu.make_async_copy(src, dst, flushes.at[len(flushed)])
        copy.start()
        flushed.append(copy)

    token_copy.wait_recv()
    row = lax.broadcasted_iota(jnp.int32, (big, 128), 0)
    natural = row // own % 2 * (2 * own) + row // (2 * own) * own + row % own
    lane = lax.broadcasted_iota(jnp.int32, (big, 128), 1)
    for block in range(2):
        at = slice(block * big, (block + 1) * big)
        angle = over_lanes(token_rows[block, 0:1]) * angles_ref[0:1]
        cos_ref[at] = jnp.cos(angle)
        sin_ref[at] = jnp.sin(angle) * angles_ref[1:2]
        starts = over_lanes(token_rows[block, 1:2])
        for c in range(big // 128):
            lanes = slice(c * 128, (c + 1) * 128)
            first = c * 128
            key = first // own % 2 * (2 * own) + first // (2 * own) * own + first % own + lane
            allowed = (starts == token_rows[block, 1:2, lanes]) & (key <= natural)
            bias_ref[block, :, lanes] = jnp.where(allowed, 0.0, -1e30).astype(BF)
    flush(cos_ref, cos_out)
    flush(sin_ref, sin_out)

    turns = [(all_rows, rows_turned, block) for block in range(width // 512)]
    turns += [(mid, mid_turned, block) for block in range(width // 512)]
    turns += [(hidden, hidden_turned, block) for block in range(hidden.shape[1] // 512)]
    turned_copies = []

    def turn():
        n = len(turned_copies)
        ref, target, block = turns[n]
        if n >= 2:
            turned_copies[-2].wait()
        at = slice(block * 512, (block + 1) * 512)
        part = ref[:, :, at].reshape(tokens, 512) if len(ref.shape) == 3 else ref[:, at]
        turning[n % 2] = jnp.transpose(part)
        copy = pltpu.make_async_copy(turning.at[n % 2], target.at[at], turn_sems.at[n])
        copy.start()
        turned_copies.append(copy)

    def load(i, into):
        stream.arrive(i)
        copy = pltpu.make_async_copy(full.at[i], into, loads.at[5 + i])
        copy.start()
        return copy

    lanes_of = lambda c, number=1: pl.ds(c * cols, number * cols)
    wide = width // gains.shape[1]
    gain_row = lambda first: jnp.concatenate([gains[r : r + 1] for r in range(first, first + wide)], axis=1)

    def rows_arrive():
        rows_gather.finish()
        for copy in gain_copies:
            copy.wait_recv()
        sums = all_gains[0].astype(F32)
        for f in range(1, count):
            sums = sums + all_gains[f].astype(F32)
        gains[...] = sums
        flush(gains, gains_out)

    def project(which):
        load(which, att_w.at[:, lanes_of(which)]).wait()

        @pl.loop(0, 4)
        def _(i):
            m = pl.ds(pl.multiple_of(i * 2 * own, 2 * own), 2 * own)
            left = all_rows[pl.ds(i * 2, 2)].reshape(2 * own, width)
            raw[m, lanes_of(which)] = product(left, att_w[:, lanes_of(which)])

    sum_copies = []

    def squares():
        parts_of = [raw[:, at : at + cols] for at in (0, cols)]
        parts_of = [jnp.sum(part * part, axis=1, keepdims=True) for part in parts_of]
        sum_copies.extend(exchange_sums(place, stats, parts_of, ssends, srecvs))
        v_low[...] = raw[:, 2 * cols :].astype(BF)
        flush(v_low, v_low_out)

    def inverses():
        inverse = lax.rsqrt(finish_sums(stats, sum_copies) / width + NORM_EPS)
        inv_ref[0] = over_lanes(inverse[0:1])
        inv_ref[1] = over_lanes(inverse[1:2])
        flush(inv_ref, inv_out)

    def rotate():
        gain_at = pl.ds(pl.multiple_of(place.pair * cols, cols), cols)

        @pl.loop(0, 8)
        def _(i):
            m = pl.ds(pl.multiple_of(i * own, own), own)
            cosine = cos_ref[m]
            sine = sin_ref[m]
            for which, hat, rot in ((0, q_hat, q_rot), (1, k_hat, k_rot)):
                inv = inv_ref[which, m]
                gain = gains[2 * wide + which : 2 * wide + which + 1, gain_at]
                for h in range(heads):
                    lanes = slice(h * HD, (h + 1) * HD)
                    value = raw[m, which * cols + h * HD : which * cols + (h + 1) * HD] * inv
                    hat[m, lanes] = value
                    value = value * gain[:, lanes]
                    value = value * cosine + pltpu.roll(value, HD // 2, 1) * sine
                    rot[m, lanes] = value.astype(BF)

        for src, dst in ((q_rot, q_rot_out), (k_rot, k_rot_out), (q_hat, q_hat_out), (k_hat, k_hat_out)):
            flush(src, dst)

    scale = HD ** (-0.5)
    quarter = big // 2

    def attend(block, i):
        h = i // 2
        lanes = pl.ds(pl.multiple_of(h * HD, HD), HD)
        q_at = pl.ds(pl.multiple_of(block * big + i % 2 * quarter, quarter), quarter)
        k_at = pl.ds(pl.multiple_of(block * big, big), big)
        b_at = pl.ds(pl.multiple_of(i % 2 * quarter, quarter), quarter)
        scores = product_last(q_rot[q_at, lanes], k_rot[k_at, lanes]) * scale + bias_ref[block, b_at].astype(F32)
        top = jnp.max(scores, axis=1, keepdims=True)
        grown = jnp.exp(scores - top)
        probs = grown / jnp.sum(grown, axis=1, keepdims=True)
        probs = probs.astype(BF)
        probs_ref[block * heads + h, b_at] = probs
        mixed[q_at, lanes] = product(probs, v_low[k_at, lanes]).astype(BF)

    attended = [0]

    def attention():
        pl.loop(0, 2 * heads)(functools.partial(attend, attended[0]))
        attended[0] += 1

    tile = tiles(mixed, att_w, parts, lanes_of(3))
    scatter = Scatter(place, tile, parts, from_core, from_chips, total, rsends, rrecvs, via=True)
    gather = Gather(place, mid, gsends, grecvs)

    def out_first():
        out_load = load(3, att_w.at[:, lanes_of(3)])
        mixed_t[...] = jnp.transpose(mixed[...])
        flush(mixed_t, mixed_turned)
        flush(probs_ref, probs_out)
        rows_gather.drain()
        out_load.wait()
        scatter.first(1)
        scatter.first(0)

    def norm():
        araw = total[...]
        inv = lax.rsqrt(jnp.mean(araw * araw, axis=1, keepdims=True) + NORM_EPS)
        normed = araw * inv
        normed_ref[...] = normed
        ainv_ref[...] = jnp.broadcast_to(inv, (own, 128))
        first_copies[2].wait()
        resid = own_rows[...].astype(F32) + normed * gain_row(0)
        resid_ref[...] = resid
        mid[mine] = resid.astype(BF)
        gather.start()
        for src, dst in ((normed_ref, normed_out), (ainv_ref, ainv_out)):
            flush(src, dst)

    loaded = {}

    def load_step(j):
        if j < steps and j not in loaded:
            at = j % 2 * 2
            loaded[j] = [load(4 + 2 * j + r, ffn_w.at[:, lanes_of(at + r)]) for r in range(2)]

    def gate_and_up(j):
        load_step(j)
        for copy in loaded[j]:
            copy.wait()
        n = slice(j * cols, (j + 1) * cols)

        @pl.loop(0, 4)
        def _(i):
            m = pl.ds(pl.multiple_of(i * 2 * own, 2 * own), 2 * own)
            left = mid[pl.ds(i * 2, 2)].reshape(2 * own, width)
            both = product(left, ffn_w[:, lanes_of(j % 2 * 2, 2)])
            gate = both[:, :cols]
            up = both[:, cols:]
            sig = jax.nn.sigmoid(gate)
            silu = gate * sig
            gate_act[m, n] = up * sig * (1.0 + gate * (1.0 - sig))
            up_act[m, n] = silu
            hidden[m, n] = (silu * up).astype(BF)

        if j == steps - 1:
            for src, dst in ((gate_act, gate_out), (up_act, up_out)):
                flush(src, dst)

    actions = {
        "k": stream.pump,
        "t": turn,
        "xr": rows_gather.relay,
        "xf": rows_arrive,
        "q0": lambda: project(0),
        "q1": lambda: project(1),
        "q2": lambda: project(2),
        "s": squares,
        "sf": inverses,
        "rope": rotate,
        "a": attention,
        "f": out_first,
        "s1": lambda: scatter.second(1),
        "s0": lambda: scatter.second(0),
        "rl": scatter.relay,
        "T": scatter.third,
        "N": norm,
        "R": gather.relay,
        "G": gather.finish,
    }
    for j in range(steps):
        actions["g%d" % j] = functools.partial(gate_and_up, j)
    each = len(stream.kinds) // 3
    for name in FORWARD_ORDER:
        if name == "k":
            stream.pump(each)
        elif name[0] == "w":
            stream.ahead = int(name[1:])
            stream.fill()
        else:
            actions[name]()

    downs = [
        load(i, att_w.at[:, lanes_of(j)]) for j, i in enumerate(range(4 + 2 * steps, len(sources)))
    ]
    for copy in downs:
        copy.wait()
    scatter.drain()
    tile = tiles(hidden, att_w, parts, lanes_of(0, steps))
    again = Scatter(place, tile, parts, from_core, from_chips, total, r2sends, r2recvs)
    again.first(1)
    again.first(0)
    again.second(1)
    again.second(0)
    top = top_ref[...].astype(F32)
    gain = gain_row(wide)
    again.third()
    fraw = total[...]
    inv = lax.rsqrt(jnp.mean(fraw * fraw, axis=1, keepdims=True) + NORM_EPS)
    normed = fraw * inv
    scaled = top * gain
    inner = jnp.mean(scaled * normed, axis=1, keepdims=True)
    all_rows[mine] = (inv * (scaled - normed * inner)).astype(BF)
    last = Gather(place, all_rows, g2sends, g2recvs, split=True)
    last.start()
    result[...] = (resid_ref[...] + normed * gain).astype(BF)
    part_gain[...] = jnp.broadcast_to(jnp.sum(top * normed, axis=0, keepdims=True), part_gain.shape)
    flush(result, output)
    flush(part_gain, part_out)
    last.relay()
    stream.drain()
    gather.drain()
    again.drain()
    for copy in sum_copies + gain_copies + [token_copy]:
        copy.wait_send()
    last.finish()
    flush(all_rows, grad_out)
    last.drain()
    for copy in flushed + turned_copies[-2:]:
        copy.wait()


def run_forward(count, rows, wq, wk, wv, wo, gate, up, down, gains, token_rows, angles, top):
    own, width = rows.shape
    tokens = 8 * own
    half = gate.shape[1] // 2
    cols = wq.shape[1] // 2
    depth = width // count
    pieces = 4 + 3 * (half // cols)
    per = pieces * (count - 1)
    shape = jax.ShapeDtypeStruct
    outs = (
        shape((pieces, width, cols), BF),
        shape(gains.shape, F32),
        shape((tokens, cols), BF), shape((tokens, cols), BF), shape((tokens, cols), BF),
        shape((tokens, cols), F32), shape((tokens, cols), F32), shape((2, tokens, 128), F32),
        shape((own, width), F32), shape((own, 128), F32),
        shape((tokens, half), F32), shape((tokens, half), F32),
        shape((own, width), BF), shape((8, width), F32), shape((2 * cols // HD, tokens // 2, tokens // 2), BF),
        shape((tokens, 128), F32), shape((tokens, 128), F32),
        shape((8, own, width), BF),
        shape((cols, tokens), BF), shape((half, tokens), BF), shape((width, tokens), BF), shape((width, tokens), BF),
    )
    scratch = lambda out: pltpu.VMEM(out.shape, out.dtype)
    return pl.pallas_call(
        functools.partial(forward_kernel, count),
        out_shape=outs,
        in_specs=[ANY] * 9 + [VMEM] * 3,
        out_specs=[ANY] * len(outs),
        scratch_shapes=[
            pltpu.VMEM((8, own, width), BF),
            pltpu.VMEM((count,) + gains.shape, BF),
            scratch(outs[1]),
            pltpu.VMEM((own, width), BF),
            pltpu.VMEM((width, max(4 * cols, half)), BF),
            pltpu.VMEM((width, 4 * cols), BF),
            pltpu.VMEM((tokens, 3 * cols), F32),
            *[scratch(out) for out in outs[2:-5]],
            scratch(outs[-4]),
            pltpu.VMEM((2, tokens // 2, tokens // 2), BF),
            pltpu.VMEM((2,) + token_rows.shape, F32),
            pltpu.VMEM((depth, 2 * cols), BF),
            pltpu.VMEM((depth, 2 * half), BF),
            pltpu.VMEM((pieces, depth, cols), BF),
            pltpu.VMEM((tokens, cols), BF),
            pltpu.VMEM((8, own, width), BF),
            pltpu.VMEM((tokens, half), BF),
            pltpu.VMEM((2, 512, tokens), BF),
            pltpu.VMEM((own, width), F32),
            pltpu.VMEM((8, 8, tokens), F32),
            pltpu.VMEM((8, own, width), BF),
            pltpu.VMEM((4, own, width), BF),
            pltpu.VMEM((3, own, width), BF),
            pltpu.VMEM((own, width), F32),
            DMA((per,)), DMA((per,)), DMA((2, pieces)), DMA((5 + pieces,)), DMA((len(outs),)),
            DMA((9,)), DMA((9,)),
            DMA((count - 1,)), DMA((count - 1,)),
            DMA((7,)), DMA((7,)),
            DMA((7,)), DMA((7,)),
            DMA((9,)), DMA((9,)),
            DMA((7,)), DMA((7,)),
            DMA((9,)), DMA((9,)),
            DMA((2 * (width // 512) + half // 512,)),
            DMA((1,)), DMA((1,)),
        ],
        compiler_params=pltpu.CompilerParams(
            collective_id=0, has_side_effects=True, vmem_limit_bytes=62 * MIB
        ),
        name="forward",
    )(rows, wq, wk, wv, wo, gate, up, down, gains, token_rows, angles, top)


COLUMN_MATRICES = (0, 3)

ORDER = (
    "d", "d", "A", "d", "f1", "p", "f0", "s1", "d", "p", "s0", "d", "p", "d", "d", "p", "d", "d",
    "p", "T", "N", "p", "d", "p", "R", "d", "p", "d", "p", "G", "D", "a", "a", "d", "r", "p", "d",
    "q", "F1", "d", "F0", "d", "p", "d", "S1", "p", "p", "p", "p", "d", "d", "p", "d", "S0", "p",
    "p", "d", "p", "d", "p", "p", "d", "p", "d", "p", "T2", "p",
)


class Collect:
    def __init__(self, place, pieces, depth, gbuf, ybuf, zbuf, ring, came, have, ready, kept, local, ysends,
                 yrecvs, zsends, zrecvs, loads, keeps):
        self.place, self.pieces, self.depth = place, pieces, depth
        columns = [matrix in COLUMN_MATRICES for matrix, _, _, _ in pieces]
        at = [columns[:p].count(columns[p]) for p in range(len(pieces))]
        self.gbuf, self.ybuf, self.zbuf = (
            [bufs[columns[p]].at[at[p]] for p in range(len(pieces))] for bufs in (gbuf, ybuf, zbuf)
        )
        self.ring = ring
        self.came, self.have, self.ready, self.kept = came, have, ready, kept
        self.loads, self.settled = loads, []
        self.made = self.launched = self.summed = 0
        self.flying = []
        self.local, self.over, self.line, self.keep = [], [], [], []
        slot = 0
        for p, (matrix, rows, wide, kind) in enumerate(pieces):
            box = (pl.ds(0, rows), pl.ds(0, wide))
            self.local.append(
                pltpu.make_async_copy(ring.at[(p % 2, slice(None)) + box], self.gbuf[p].at[(slice(None),) + box], local.at[p])
            )
            self.over.append(
                send(
                    self.gbuf[p].at[(1 - place.low,) + box],
                    self.ybuf[p].at[box],
                    ysends,
                    yrecvs,
                    p,
                    place.across(),
                )
            )
            self.keep.append(
                pltpu.make_async_copy(self.gbuf[p].at[(place.low,) + box], have.at[box], loads.at[0])
            )
            if kind == (0, 0):
                self.line.append(None)
                self.settled.append(
                    pltpu.make_async_copy(kept[matrix], self.zbuf[p].at[box], keeps.at[len(self.settled)])
                )
                continue
            self.line.append(
                send(
                    ready.at[(slot % ready.shape[0],) + box],
                    self.zbuf[p].at[box],
                    zsends,
                    zrecvs,
                    p,
                    place.line(*kind),
                )
            )
            slot += 1

    def owner(self, p):
        both = 2 * self.depth
        return pl.ds(pl.multiple_of(self.place.high_at(*self.pieces[p][3]) * both, both), both)

    def make_rows(self, left, right, first):
        p = self.made
        self.launch()
        ring = self.ring.at[p % 2]
        wide = self.pieces[p][2]
        step = 512 if wide % 512 == 0 else 256

        @pl.loop(0, wide // step)
        def _(n):
            lanes = pl.ds(pl.multiple_of(first + n * step, step), step)
            to = pl.ds(pl.multiple_of(n * step, step), step)
            out = product(left[...], right[:, lanes]).astype(BF)
            ring[0, : self.depth, to] = out[: self.depth]
            ring[1, : self.depth, to] = out[self.depth :]

        self.local[p].start()
        self.made = p + 1

    def make_columns(self, left, right):
        p = self.made
        self.launch()
        ring = self.ring.at[p % 2]
        _, rows, wide, _ = self.pieces[p]
        number = left.shape[0] // rows
        pitch = wide // number
        tokens = right.shape[0] * right.shape[1]
        cols = right[:, :, self.owner(p)].reshape(tokens, 2 * self.depth)
        together = 2 if number % 2 == 0 else 1
        for c in range(0, number, together):
            out = product(left[c * rows : (c + together) * rows], cols).astype(BF)
            for r in range(together):
                for low in (0, 1):
                    ring[low, :rows, (c + r) * pitch : (c + r) * pitch + self.depth] = out[
                        r * rows : (r + 1) * rows, low * self.depth : (low + 1) * self.depth
                    ]
        self.local[p].start()
        self.made = p + 1

    def launch(self):
        while self.launched < self.made:
            self.local[self.launched].wait()
            self.over[self.launched].start()
            self.launched += 1

    def pump(self, number=1):
        self.launch()
        for _ in range(number):
            p = self.summed
            if p >= self.made:
                return
            matrix, rows, wide, kind = self.pieces[p]
            box = (slice(0, rows), slice(0, wide))
            self.keep[p].start()
            self.over[p].wait_recv()
            came = pltpu.make_async_copy(
                self.ybuf[p].at[pl.ds(0, rows), pl.ds(0, wide)],
                self.came.at[pl.ds(0, rows), pl.ds(0, wide)],
                self.loads.at[2],
            )
            came.start()
            self.keep[p].wait()
            came.wait()
            total = self.came[box].astype(F32) + self.have[box].astype(F32)
            if kind == (0, 0):
                self.kept[matrix][...] = total.astype(BF)
                self.settled[matrix].start()
            else:
                slots = self.ready.shape[0]
                if len(self.flying) >= slots:
                    self.flying[-slots].wait_send()
                self.ready[(len(self.flying) % slots,) + box] = total.astype(BF)
                self.line[p].start()
                self.flying.append(self.line[p])
            self.summed = p + 1

    def drain(self):
        for copy in self.over:
            copy.wait_send()
        for copy in self.flying[-self.ready.shape[0] :]:
            copy.wait_send()
        for copy in self.line:
            if copy is not None:
                copy.wait_recv()
        for copy in self.settled:
            copy.wait()


def backward_kernel(
    count, pieces,
    gffn_in, hidden_in, gate_in, up_in, mid_in, rows_in, full, mixed_in, q_in, k_in, v_in, qh_in, kh_in, inv_in,
    cos_in, sin_in, probs_in, normed_ref, ainv_ref, top_ref, gains_ref, pgain_ref,
    grad_rows, gain_sums,
    gbuf_r, gbuf_c, ybuf_r, ybuf_c, zbuf_r, zbuf_c,
    rows_a, rows_c, hidden, acts, floats, weights, parts, from_core, from_chips, total, resid, turned, ring,
    came, have, ready, kept0, kept1, kept2, kept3, kept4, kept5,
    mixed, q_rot, k_rot, v_low, q_hat, k_hat, inv, cos_ref, sin_ref, probs_ref, datt, dqkv, stats, side_sums, all_sums,
    big_loads, loads, local, ysends, yrecvs, zsends, zrecvs, rsends, rrecvs, r2sends, r2recvs, gsends, grecvs,
    ssends, srecvs, xsends, xrecvs, fsends, frecvs, keeps,
):
    place = Place(count)
    own, width = top_ref.shape
    tokens = 8 * own
    big = tokens // 2
    cols = mixed.shape[0]
    heads = cols // HD
    steps = hidden.shape[0] // cols
    depth = width // count
    others = [(place.index + step) % count for step in range(1, count)]
    tensor_peers = [(0, 1), (1, 0), (1, 1)]

    used = [0]

    def load(src, into):
        copy = pltpu.make_async_copy(src, into, big_loads.at[used[0]])
        used[0] += 1
        copy.start()
        return copy

    def chunk(ref, j):
        return ref.at[:, pl.ds(j * cols, cols)]

    rows_load = load(gffn_in, rows_a)
    hidden_load = load(hidden_in, hidden)
    firsts = [
        [
            load(full.at[4 + 2 * steps + j], chunk(weights, j)),
            load(chunk(gate_in, j), floats.at[2 * (j % 2)]),
            load(chunk(up_in, j), floats.at[2 * (j % 2) + 1]),
        ]
        for j in range(min(2, steps))
    ]
    for j in range(2, steps):
        firsts.append([load(full.at[4 + 2 * steps + j], chunk(weights, j))])
    greet(
        [{"fsdp": other, "tensor": place.tensor} for other in others]
        + [place.peer(p, c, s) for p, c, s in place.group() if c or s]
    )
    kept = [kept0, kept1, kept2, kept3, kept4, kept5]
    collect = Collect(
        place, pieces, depth, (gbuf_r, gbuf_c), (ybuf_r, ybuf_c), (zbuf_r, zbuf_c), ring, came, have, ready, kept, local,
        ysends, yrecvs, zsends, zrecvs, loads, keeps,
    )
    number = len(place.lines()) + 1

    wanted = [(mid_in, number + 2 * k) for k in range(number)] + [
        (rows_in, (4 + turn) * number + k) for turn in range(2) for k in range(number)
    ]
    blocks = []

    def next_block():
        i = len(blocks)
        if i < len(wanted):
            ref, p = wanted[i]
            blocks.append(load(ref.at[collect.owner(p)], turned.at[i % 2]))

    next_block()
    next_block()
    waited = set()

    def once(*copies):
        for copy in copies:
            if id(copy) not in waited:
                waited.add(id(copy))
                copy.wait()

    def make_down():
        once(rows_load, hidden_load)
        collect.make_columns(hidden, rows_a)

    def make_rows(i, right, first, last):
        once(blocks[i])
        collect.make_rows(turned.at[i % 2], right, first)
        if last:
            next_block()

    makes = [make_down] * number
    for k in range(number):
        makes.append(functools.partial(make_rows, k, acts, 0, False))
        makes.append(functools.partial(make_rows, k, acts, steps * cols, True))
    def make_out():
        once(*late["rest"])
        collect.make_columns(mixed, rows_c)

    makes += [make_out] * number
    for turn, first in ((1, 2 * cols), (2, 0)):
        for k in range(number):
            makes.append(functools.partial(make_rows, turn * number + k, dqkv, first, True))

    late = {}

    def gate_and_up():
        once(rows_load)
        for j in range(steps):
            once(*firsts[j])
            at = 2 * (j % 2)

            @pl.loop(0, 2)
            def _(i):
                m = pl.ds(pl.multiple_of(i * big, big), big)
                left = rows_a[pl.ds(i * 4, 4)].reshape(big, width)
                grad = product(left, weights[:, j * cols : (j + 1) * cols])
                acts[m, 2 * j * cols : (2 * j + 1) * cols] = (grad * floats[at, m]).astype(BF)
                acts[m, (2 * j + 1) * cols : (2 * j + 2) * cols] = (grad * floats[at + 1, m]).astype(BF)

            if j + 2 < steps:
                firsts[j + 2] += [
                    load(chunk(gate_in, j + 2), floats.at[at]),
                    load(chunk(up_in, j + 2), floats.at[at + 1]),
                ]
        late["ffn"] = [load(full.at[4 + c], chunk(weights, c)) for c in range(2 * steps)]
        late["rest"] = [
            load(src, into)
            for src, into in (
                (mixed_in, mixed), (q_in, q_rot), (k_in, k_rot), (v_in, v_low), (qh_in, q_hat), (kh_in, k_hat),
                (inv_in, inv), (cos_in, cos_ref), (sin_in, sin_ref), (probs_in, probs_ref),
            )
        ]

    tile = tiles(acts, weights, parts, pl.ds(0, acts.shape[1]))
    scatter = Scatter(place, tile, parts, from_core, from_chips, total, rsends, rrecvs, via=True)
    tile = tiles(dqkv, weights, parts, pl.ds(0, 3 * cols))
    again = Scatter(place, tile, parts, from_core, from_chips, total, r2sends, r2recvs, via=True)
    gather = Gather(place, rows_c, gsends, grecvs)
    wide = width // gains_ref.shape[1]
    lanes_per = gains_ref.shape[1]
    cut = lambda row: [row[:, r * lanes_per : (r + 1) * lanes_per] for r in range(wide)]
    side_copies, inner_copies, all_copies = [], [], []

    def first(pair):
        once(*late["ffn"])
        scatter.first(pair)

    def second(pair):
        scatter.second(pair)
        if not pair:
            scatter.relay()
            late["att"] = [load(full.at[c], chunk(weights, c)) for c in range(4)]

    def norm():
        normed = normed_ref[...]
        gain = jnp.concatenate([gains_ref[r : r + 1] for r in range(wide)], axis=1)
        grad = top_ref[...].astype(F32) + total[...]
        resid[...] = grad
        part_gain = jnp.sum(grad * normed, axis=0, keepdims=True)
        scaled = grad * gain
        inner = jnp.mean(scaled * normed, axis=1, keepdims=True)
        rows_c[place.slot()] = (ainv_ref[:, :1] * (scaled - normed * inner)).astype(BF)
        gather.start()
        side_sums[place.tensor] = jnp.concatenate(cut(part_gain) + cut(pgain_ref[0:1]), axis=0)
        for i, (c, s) in enumerate(tensor_peers):
            copy = send(
                side_sums.at[place.tensor], side_sums.at[place.tensor], xsends, xrecvs, i, place.peer(0, c, s)
            )
            copy.start()
            side_copies.append(copy)

    def out_back():
        once(*late["att"], *late["rest"])

        @pl.loop(0, 2)
        def _(i):
            m = pl.ds(pl.multiple_of(i * big, big), big)
            left = rows_c[pl.ds(i * 4, 4)].reshape(big, width)
            datt[m] = product(left, weights[:, 3 * cols : 4 * cols]).astype(BF)

    scale = HD ** (-0.5)
    quarter = big // 2

    def attend(block, h):
        lanes = pl.ds(pl.multiple_of(h * HD, HD), HD)
        k_at = pl.ds(pl.multiple_of(block * big, big), big)
        keys = k_rot[k_at, lanes]
        values = v_low[k_at, lanes]
        for half in range(2):
            q_at = pl.ds(pl.multiple_of(block * big + half * quarter, quarter), quarter)
            queries = q_rot[q_at, lanes]
            grads = datt[q_at, lanes]
            low = probs_ref[block * heads + h, half * quarter : (half + 1) * quarter]
            probs = low.astype(F32)
            dprobs = product_last(grads, values)
            inner = jnp.sum(probs * dprobs, axis=1, keepdims=True)
            dscores = (probs * (dprobs - inner)).astype(BF)
            floats[0, q_at, lanes] = product(dscores, keys) * scale
            dkeys = product_first(dscores, queries) * scale
            dvalues = product_first(low, grads)
            if half:
                floats[1, k_at, lanes] += dkeys
                floats[2, k_at, lanes] += dvalues
            else:
                floats[1, k_at, lanes] = dkeys
                floats[2, k_at, lanes] = dvalues

    attended = [0]

    def attention():
        pl.loop(0, heads)(functools.partial(attend, attended[0]))
        m = pl.ds(attended[0] * big, big)
        dqkv[m, 2 * cols :] = floats[2, m].astype(BF)
        attended[0] += 1

    def rotate_back():
        gain_at = pl.ds(pl.multiple_of(place.pair * cols, cols), cols)
        norm_gains = [gains_ref[2 * wide + which : 2 * wide + which + 1, gain_at] for which in (0, 1)]
        gain_parts, inners = [], []
        for which, hat in ((0, q_hat), (1, k_hat)):
            pieces_of = []
            for h in range(heads):
                lanes = slice(h * HD, (h + 1) * HD)
                value = floats[which, :, lanes]
                value = value * cos_ref[...] - pltpu.roll(value, HD // 2, 1) * sin_ref[...]
                weighted = value * hat[:, lanes]
                gain_parts.append(jnp.sum(weighted, axis=0, keepdims=True))
                part = norm_gains[which][:, lanes]
                pieces_of.append(jnp.sum(weighted * part, axis=1, keepdims=True))
                floats[which, :, lanes] = value * part
            inners.append(sum(pieces_of[1:], pieces_of[0]))
        inner_copies.extend(exchange_sums(place, stats, inners, ssends, srecvs))
        for copy in side_copies:
            copy.wait_recv()
        side = side_sums[0]
        for t in range(1, side_sums.shape[0]):
            side = side + side_sums[t]
        gain_rows = [jnp.concatenate(gain_parts[w * heads : (w + 1) * heads], axis=1) for w in (0, 1)]
        upper = place.pair == 1
        gain_rows = [
            jnp.concatenate([jnp.where(upper, 0.0, row), jnp.where(upper, row, 0.0)], axis=1) for row in gain_rows
        ]
        spare = jnp.zeros((all_sums.shape[1] - 2 * wide - 2, lanes_per), F32)
        all_sums[place.index] = jnp.concatenate([side] + gain_rows + [spare], axis=0)
        for i, other in enumerate(others):
            copy = send(
                all_sums.at[place.index], all_sums.at[place.index], fsends, frecvs, i,
                {"fsdp": other, "tensor": place.tensor},
            )
            copy.start()
            all_copies.append(copy)

    def query_key():
        sums = finish_sums(stats, inner_copies) / width
        for which, hat in ((0, q_hat), (1, k_hat)):
            lanes_inner = over_lanes(sums[which : which + 1])
            for h in range(heads):
                lanes = slice(h * HD, (h + 1) * HD)
                value = inv[which] * (floats[which, :, lanes] - hat[:, lanes] * lanes_inner)
                dqkv[:, which * cols + h * HD : which * cols + (h + 1) * HD] = value.astype(BF)

    def first_again(pair):
        if pair:
            scatter.drain()
        again.first(pair)

    def second_again(pair):
        again.second(pair)
        if not pair:
            again.relay()

    grad_copies = []

    def third_again():
        again.third()
        total[...] += resid[...]
        grad_copies.append(load(total, grad_rows))

    actions = {
        "A": gate_and_up,
        "f1": lambda: first(1),
        "f0": lambda: first(0),
        "s1": lambda: second(1),
        "s0": lambda: second(0),
        "T": scatter.third,
        "N": norm,
        "R": gather.relay,
        "G": gather.finish,
        "D": out_back,
        "a": attention,
        "r": rotate_back,
        "q": query_key,
        "F1": lambda: first_again(1),
        "F0": lambda: first_again(0),
        "S1": lambda: second_again(1),
        "S0": lambda: second_again(0),
        "T2": third_again,
    }
    each = number // 4
    for name in ORDER:
        if name == "d":
            for _ in range(each):
                makes.pop(0)()
        elif name == "p":
            collect.pump(each)
        else:
            actions[name]()
    for copy in all_copies:
        copy.wait_recv()
    sums = all_sums[0]
    for f in range(1, count):
        sums = sums + all_sums[f]
    gain_sums[...] = sums
    for copy in grad_copies:
        copy.wait()
    collect.drain()
    again.drain()
    gather.drain()
    for copy in inner_copies + side_copies + all_copies:
        copy.wait_send()


def list_pieces(count, depth, cols, half):
    kinds = line_kinds(count) + [(0, 0)]
    pitch = max(depth, 128)
    sizes = [
        (cols, half // cols * pitch), (depth, half), (depth, half), (cols, pitch), (depth, cols), (depth, 2 * cols),
    ]
    order = [[0], [1, 2], [3], [4], [5]]
    return sizes, [(m,) + sizes[m] + (kind,) for group in order for kind in kinds for m in group]


def settle_kernel(
    pieces, zbuf_r, zbuf_c, grad_in, out_in,
    out_q, out_k, out_v, out_o, out_gate, out_up, out_down, grad_out, out_out,
    boxes_r, boxes_c, grad_held, out_held, stage0, stage1, stage2, stage3, stage4, stage5, loads, stores, copies,
):
    stages = [stage0, stage1, stage2, stage3, stage4, stage5]
    whole = []
    for i, (src, held_here, dst) in enumerate(((grad_in, grad_held, grad_out), (out_in, out_held, out_out))):
        into = pltpu.make_async_copy(src, held_here, copies.at[i])
        into.start()
        whole.append((into, pltpu.make_async_copy(held_here, dst, copies.at[2 + i])))
    pair = lax.axis_index("fsdp") // 2 % 2
    held, count = [], [0, 0]
    for p, (matrix, _, _, _) in enumerate(pieces):
        column = matrix in COLUMN_MATRICES
        at = count[column]
        count[column] += 1
        zbuf, boxes = (zbuf_c, boxes_c) if column else (zbuf_r, boxes_r)
        _, rows, wide, _ = pieces[p]
        box = (pl.ds(0, rows), pl.ds(0, wide))
        copy = pltpu.make_async_copy(zbuf.at[(at,) + box], boxes.at[(at,) + box], loads.at[p])
        copy.start()
        held.append((copy, boxes, at))
    for into, back in whole:
        into.wait()
        back.start()
    cols = out_q.shape[1] // 2
    steps = out_gate.shape[1] // 2 // cols
    both = [(ref, j * cols) for j in range(steps) for ref in (out_gate, out_up)]
    groups = [
        [(out_down, None)] * steps,
        both[:steps],
        both[steps:],
        [(out_o, None)],
        [(out_v, 0)],
        [(out_q, 0), (out_k, 0)],
    ]
    sent = []
    for matrix, targets in enumerate(groups):
        for p, (m, _, _, _) in enumerate(pieces):
            if m == matrix:
                held[p][0].wait()
        stage = stages[matrix]
        rows, wide = stage.shape[1:]
        step = min(rows, 64)

        @pl.loop(0, rows // step)
        def _(i):
            at = pl.ds(pl.multiple_of(i * step, step), step)
            sums = [None, None]
            for p, (m, _, _, kind) in enumerate(pieces):
                if m != matrix:
                    continue
                _, boxes, index = held[p]
                part = boxes[index, at, :wide].astype(F32)
                which = kind[1]
                sums[which] = part if sums[which] is None else sums[which] + part
            stage[0, at] = sums[0]
            stage[1, at] = sums[1]

        pitch = wide // len(targets)
        for r in (0, 1):
            half = flip(pair, r)
            for c, (ref, at) in enumerate(targets):
                src = stage.at[r, :, pl.ds(c * pitch, pitch)]
                if at is None:
                    start = half * (ref.shape[0] // 2) + c * rows
                    dst = ref.at[pl.ds(pl.multiple_of(start, rows), rows)]
                else:
                    start = half * (ref.shape[1] // 2) + at
                    dst = ref.at[:, pl.ds(pl.multiple_of(start, pitch), pitch)]
                copy = pltpu.make_async_copy(src, dst, stores.at[len(sent)])
                copy.start()
                sent.append(copy)
    for copy in sent + [back for _, back in whole]:
        copy.wait()


def run_settle(count, cols, half, zbuf_r, zbuf_c, grad, output):
    width = grad.shape[1]
    depth = width // count
    sizes, pieces = list_pieces(count, depth, cols, half)
    pitch = max(depth, 128)
    shape = jax.ShapeDtypeStruct
    small = shape((depth, 2 * cols), F32)
    large = shape((depth, 2 * half), F32)
    outs = (
        small, small, small, shape((2 * cols, pitch), F32),
        large, large, shape((2 * half, pitch), F32),
        shape(grad.shape, grad.dtype), shape(output.shape, output.dtype),
    )
    return pl.pallas_call(
        functools.partial(settle_kernel, pieces),
        out_shape=outs,
        in_specs=[ANY] * 4,
        out_specs=[ANY] * len(outs),
        scratch_shapes=[
            pltpu.VMEM(zbuf_r.shape, BF),
            pltpu.VMEM(zbuf_c.shape, BF),
            pltpu.VMEM(grad.shape, grad.dtype),
            pltpu.VMEM(output.shape, output.dtype),
            *[pltpu.VMEM((2,) + size, F32) for size in sizes],
            DMA((len(pieces),)), DMA((64,)), DMA((4,)),
        ],
        compiler_params=pltpu.CompilerParams(vmem_limit_bytes=62 * MIB),
        name="settle",
    )(zbuf_r, zbuf_c, grad, output)


def run_backward(
    count, gffn, hidden, gate, up, mid, rows, full, mixed, q_rot, k_rot, v_low, q_hat, k_hat, inv, cosine, sine, probs,
    normed, ainv, top, gains, part_gain,
):
    own, width = top.shape
    tokens = 8 * own
    cols = mixed.shape[0]
    half = hidden.shape[0]
    depth = width // count
    steps = half // cols
    pitch = max(depth, 128)
    kinds = line_kinds(count) + [(0, 0)]
    sizes, pieces = list_pieces(count, depth, cols, half)
    number = len(pieces)
    kinds_of = ((4 * len(kinds), sizes[1]), (2 * len(kinds), sizes[0]))
    box = (max(depth, cols), half)
    shape = jax.ShapeDtypeStruct
    outs = (
        shape((own, width), F32),
        shape(gains.shape, F32),
        *[shape((n,) + lead + size, BF) for lead in ((2,), (), ()) for n, size in kinds_of],
    )
    like = lambda array: pltpu.VMEM(array.shape, array.dtype)
    return pl.pallas_call(
        functools.partial(backward_kernel, count, pieces),
        out_shape=outs,
        in_specs=[ANY] * 17 + [VMEM] * 5,
        out_specs=[ANY, VMEM] + [ANY] * 6,
        scratch_shapes=[
            like(gffn), like(gffn), like(hidden),
            pltpu.VMEM((tokens, 2 * half), BF),
            pltpu.VMEM((4, tokens, cols), F32),
            pltpu.VMEM((width, 2 * half), BF),
            pltpu.VMEM((8, own, width), BF),
            pltpu.VMEM((4, own, width), BF),
            pltpu.VMEM((3, own, width), BF),
            pltpu.VMEM((own, width), F32),
            pltpu.VMEM((own, width), F32),
            pltpu.VMEM((2, 2 * depth, tokens), BF),
            pltpu.VMEM((2, 2) + box, BF),
            pltpu.VMEM(box, BF),
            pltpu.VMEM(box, BF),
            pltpu.VMEM((6,) + box, BF),
            *[pltpu.VMEM(size, BF) for size in sizes],
            like(mixed), like(q_rot), like(k_rot), like(v_low), like(q_hat), like(k_hat), like(inv),
            like(cosine), like(sine), like(probs),
            pltpu.VMEM((tokens, cols), BF),
            pltpu.VMEM((tokens, 3 * cols), BF),
            pltpu.VMEM((8, 8, tokens), F32),
            pltpu.VMEM((4, 2 * width // gains.shape[1], gains.shape[1]), F32),
            pltpu.VMEM((count,) + gains.shape, F32),
            DMA((64 + 3 * len(kinds),)), DMA((3,)), DMA((number,)),
            DMA((number,)), DMA((number,)),
            DMA((number,)), DMA((number,)),
            DMA((7,)), DMA((7,)),
            DMA((7,)), DMA((7,)),
            DMA((9,)), DMA((9,)),
            DMA((7,)), DMA((7,)),
            DMA((3,)), DMA((3,)),
            DMA((count - 1,)), DMA((count - 1,)),
            DMA((6,)),
        ],
        compiler_params=pltpu.CompilerParams(
            collective_id=1, has_side_effects=True, vmem_limit_bytes=63 * MIB
        ),
        name="backward",
    )(
        gffn, hidden, gate, up, mid, rows, full, mixed, q_rot, k_rot, v_low, q_hat, k_hat, inv, cosine, sine, probs,
        normed, ainv, top, gains, part_gain,
    )


def local(
    inputs,
    seg_ids,
    positions,
    w_query,
    w_key,
    w_value,
    w_out,
    query_gain,
    key_gain,
    attn_gain,
    w_gate,
    w_up,
    w_down,
    ffn_gain,
    out_grad,
    count,
    tensor,
):
    index = lax.axis_index("fsdp")
    own_rows, width = inputs.shape
    group_rows = seg_ids.shape[0]
    depth = width // count

    heads_here, part = query_gain.shape
    heads_half = heads_here // 2
    cols = heads_half * HD
    sizes = heads_here * part

    def placed(values, copies):
        size = values.shape[-1]
        here = jnp.arange(size * count, dtype=jnp.int32) // size == index
        return jnp.where(here, jnp.tile(values, copies), 0).reshape(-1, heads_here * HD)

    packed = jnp.concatenate(
        [
            placed(attn_gain, count),
            placed(ffn_gain, count),
            placed(jnp.concatenate([query_gain, key_gain]), (1, count)),
        ]
    )
    packed = jnp.pad(packed, ((0, -packed.shape[0] % 16), (0, 0)))

    token_rows = jnp.pad(jnp.stack([positions, seg_ids]).astype(F32), ((0, 6), (0, 0)))
    freq = np.float32(ROPE_THETA) ** (-(np.arange(HD // 2, dtype=np.float32) * 2) / np.float32(HD))
    angles = np.zeros((8, HD), np.float32)
    angles[0] = np.concatenate([freq, freq])
    angles[1] = np.concatenate([-np.ones(HD // 2), np.ones(HD // 2)])
    turned = depth % 128 != 0

    (
        full, gains, query_rot, key_rot, value_low, query_hat, key_hat, invs, attn_normed, attn_inv, gate_raw, up_raw,
        output, partial_ffn_gain, probs, cosine, sine, rows_grad_ffn, mixed_low, hidden_low, all_rows, rows_mid,
    ) = run_forward(
        count, inputs, w_query, w_key, w_value, w_out.T if turned else w_out, w_gate, w_up,
        w_down.T if turned else w_down, packed, token_rows, angles, out_grad,
    )
    wide = width // gains.shape[1]
    (
        grad_rows, gain_sums, _, _, _, _, zbuf_r, zbuf_c,
    ) = run_backward(
        count, rows_grad_ffn, hidden_low, gate_raw, up_raw, rows_mid, all_rows, full, mixed_low, query_rot,
        key_rot, value_low, query_hat, key_hat, invs, cosine, sine, probs, attn_normed, attn_inv,
        out_grad, gains, partial_ffn_gain,
    )

    (
        sum_query, sum_key, sum_value, sum_out, sum_gate, sum_up, sum_down, grad_inputs, output,
    ) = run_settle(count, cols, hidden_low.shape[0], zbuf_r, zbuf_c, grad_rows, output)

    def own_gain(row):
        return lax.dynamic_slice_in_dim(gain_sums[row * wide : (row + 1) * wide].reshape(-1), index * depth, depth)

    def own_head_gain(row):
        values = gain_sums[2 * wide + row].reshape(heads_here, HD)
        return lax.dynamic_slice_in_dim(values, index * part, part, 1)

    return (
        output,
        grad_inputs,
        sum_query,
        sum_key,
        sum_value,
        sum_out[:, :depth],
        own_head_gain(0),
        own_head_gain(1),
        own_gain(0),
        sum_gate,
        sum_up,
        sum_down[:, :depth],
        own_gain(1),
    )


def solution(mesh):
    count = mesh.shape["fsdp"]
    tensor = mesh.shape["tensor"]
    tokens = P(("fsdp", "tensor"), None)
    rows = P("fsdp", "tensor")
    columns = P("tensor", "fsdp")
    line = P("fsdp")

    def body(*arrays):
        return local(*arrays, count=count, tensor=tensor)

    return jax.shard_map(
        body,
        mesh=mesh,
        in_specs=(
            tokens, line, line, rows, rows, rows, columns, columns, columns, line,
            rows, rows, columns, line, tokens,
        ),
        out_specs=(
            tokens, tokens, rows, rows, rows, columns, columns, columns, line,
            rows, rows, columns, line,
        ),
        check_vma=False,
    )
```

```python
import functools

import jax
import jax.numpy as jnp
import numpy as np
from jax import lax
from jax.experimental import pallas as pl
from jax.experimental.pallas import tpu as pltpu
from jax.sharding import PartitionSpec as P

HD = 128
NORM_EPS = 1e-06
ROPE_THETA = 500000.0
BF = jnp.bfloat16
F32 = jnp.float32
MIB = 1 << 20


class Place:
    def __init__(self, count):
        self.count = count
        self.outers = count // 4
        self.index = lax.axis_index("fsdp")
        self.tensor = lax.axis_index("tensor")
        self.low = self.index % 2
        self.high = self.index // 2
        self.pair = self.high % 2
        self.outer = self.high // 2
        self.core = self.tensor % 2
        self.side = self.tensor // 2

    def device(self, outer, pair, low, core, side):
        return {"fsdp": (outer * 2 + pair) * 2 + low, "tensor": side * 2 + core}

    def peer(self, pair=0, core=0, side=0):
        return self.device(
            self.outer, flip(self.pair, pair), self.low, flip(self.core, core), flip(self.side, side)
        )

    def slot(self, pair=0, core=0, side=0):
        return flip(self.pair, pair) * 4 + flip(self.core, core) * 2 + flip(self.side, side)

    def line(self, step, pair):
        outer = (self.outer + step) % self.outers
        return self.device(outer, flip(self.pair, pair), self.low, self.core, self.side)

    def high_at(self, step, pair):
        return ((self.outer + step + self.outers) % self.outers) * 2 + flip(self.pair, pair)

    def across(self):
        return self.device(self.outer, self.pair, 1 - self.low, self.core, self.side)

    def lines(self):
        return line_kinds(self.count)

    def group(self):
        return [(p, c, s) for p in (0, 1) for c in (0, 1) for s in (0, 1) if p or c or s]


def line_kinds(count):
    return [(step, pair) for step in reversed(range(count // 4)) for pair in (0, 1) if step or pair]


def flip(bit, yes):
    return 1 - bit if yes else bit


def greet(devices):
    barrier = pltpu.get_barrier_semaphore()
    for device in devices:
        pl.semaphore_signal(barrier, inc=1, device_id=device, device_id_type=pl.DeviceIdType.MESH)
    pl.semaphore_wait(barrier, len(devices))


def send(src, dst, sends, recvs, slot, device):
    return pltpu.make_async_remote_copy(
        src_ref=src,
        dst_ref=dst,
        send_sem=sends.at[slot],
        recv_sem=recvs.at[slot],
        device_id=device,
        device_id_type=pl.DeviceIdType.MESH,
    )


def product(left, right):
    return lax.dot_general(left, right, (((1,), (0,)), ((), ())), preferred_element_type=F32)


def product_last(left, right):
    return lax.dot_general(left, right, (((1,), (1,)), ((), ())), preferred_element_type=F32)


def product_first(left, right):
    return lax.dot_general(left, right, (((0,), (0,)), ((), ())), preferred_element_type=F32)


class Gather:
    slots = 9

    def __init__(self, place, rows, sends, recvs, split=False):
        half = rows.shape[1] // 2

        def go(slot, device, part=None, **kw):
            ref = rows.at[place.slot(**kw)]
            if part is not None:
                ref = rows.at[place.slot(**kw), pl.ds(part * half, half)]
            return send(ref, ref, sends, recvs, slot, place.peer(**device))

        self.to_pair = go(0, dict(pair=1))
        self.to_side = go(1, dict(side=1))
        self.to_core = go(2, dict(core=1))
        self.pair_to_core = go(5, dict(core=1), pair=1)
        self.side_to_core = go(6, dict(core=1), side=1)
        if split:
            self.relays = [go(3, dict(side=1), 0, pair=1), go(4, dict(pair=1), 1, side=1)]
            self.last = [go(7, dict(core=1), 0, pair=1, side=1), go(8, dict(core=1), 1, pair=1, side=1)]
        else:
            self.relays = [go(3, dict(side=1), pair=1)]
            self.last = [go(7, dict(core=1), pair=1, side=1)]

    def start(self):
        self.to_pair.start()
        self.to_side.start()
        self.to_core.start()

    def relay(self):
        self.to_pair.wait_recv()
        self.relays[0].start()
        self.pair_to_core.start()
        self.to_side.wait_recv()
        for copy in self.relays[1:]:
            copy.start()
        self.side_to_core.start()

    def finish(self):
        for relay, copy in zip(self.relays, self.last):
            relay.wait_recv()
            copy.start()
        for copy in [self.to_core, self.pair_to_core, self.side_to_core] + self.last:
            copy.wait_recv()

    def drain(self):
        for copy in [self.to_pair, self.to_side, self.to_core, self.pair_to_core, self.side_to_core]:
            copy.wait_send()
        for copy in self.relays + self.last:
            copy.wait_send()


class Scatter:
    order = [(1, 1), (1, 0), (0, 1), (0, 0)]

    def __init__(self, place, tile, parts, from_core, from_chips, total, sends, recvs, via=False):
        self.place, self.tile, self.parts = place, tile, parts
        self.from_core, self.from_chips, self.total, self.via = from_core, from_chips, total, via
        self.to_core = [
            send(
                parts.at[place.slot(pair=pair, core=1, side=side)],
                from_core.at[slot],
                sends,
                recvs,
                slot,
                place.peer(core=1),
            )
            for slot, (pair, side) in enumerate(self.order)
        ]
        self.to_chips = [
            send(
                parts.at[place.slot(pair=pair, side=side)],
                from_chips.at[slot],
                sends,
                recvs,
                4 + slot,
                place.peer(pair=pair if slot or not via else 0, side=side),
            )
            for slot, (pair, side) in enumerate(self.order[:3])
        ]

    def first(self, pair):
        place = self.place
        self.tile(flip(place.pair, pair), 1 - place.core)
        for slot, (p, side) in enumerate(self.order):
            if p == pair:
                self.to_core[slot].start()

    def both(self, slot):
        pair, side = self.order[slot]
        mine = self.place.slot(pair=pair, side=side)
        return mine, self.parts[mine].astype(F32) + self.from_core[slot].astype(F32)

    def second(self, pair):
        self.tile(flip(self.place.pair, pair), self.place.core)
        for slot, (p, side) in enumerate(self.order):
            if p != pair:
                continue
            self.to_core[slot].wait_recv()
            if self.via and slot == 1:
                continue
            mine, both = self.both(slot)
            if slot < 3:
                self.parts[mine] = both.astype(BF)
                self.to_chips[slot].start()
            else:
                self.total[...] = both

    def relay(self):
        if self.via:
            self.to_chips[0].wait_recv()
            mine, both = self.both(1)
            self.parts[mine] = (both + self.from_chips[0].astype(F32)).astype(BF)
            self.to_chips[1].start()

    def third(self):
        for slot, copy in enumerate(self.to_chips):
            if slot or not self.via:
                copy.wait_recv()
                self.total[...] += self.from_chips[slot].astype(F32)

    def drain(self):
        for copy in self.to_core + self.to_chips:
            copy.wait_send()


def tiles(left_ref, right, parts, lanes):
    own, width = parts.shape[1:]

    def tile(pair, core):
        first = pair * 4 + core * 2
        m = pl.ds(pl.multiple_of(first * own, 2 * own), 2 * own)

        @pl.loop(0, width // 512)
        def _(n):
            at = pl.ds(pl.multiple_of(n * 512, 512), 512)
            out = product_last(left_ref[m, :], right[at, lanes]).astype(BF)
            parts[first, :, at] = out[:own]
            parts[first + 1, :, at] = out[own:]

    return tile


def exchange_sums(place, stats, columns, sends, recvs):
    tokens = stats.shape[2]
    rows = [jnp.transpose(jnp.broadcast_to(column, (tokens, 128)))[0:1] for column in columns]
    stats[place.slot()] = jnp.concatenate(rows + [jnp.zeros((6, tokens), F32)], axis=0)
    return exchange_rows(place, stats, sends, recvs)


def exchange_rows(place, stats, sends, recvs):
    mine = place.slot()
    copies = []
    for i, (p, c, s) in enumerate(place.group()):
        copy = send(stats.at[mine], stats.at[mine], sends, recvs, i, place.peer(p, c, s))
        copy.start()
        copies.append(copy)
    return copies


def finish_sums(stats, copies):
    for copy in copies:
        copy.wait_recv()
    sums = stats[0]
    for g in range(1, 8):
        sums = sums + stats[g]
    return sums


def over_lanes(row):
    return jnp.transpose(jnp.broadcast_to(row, (128, row.shape[1])))


class Stream:
    def __init__(self, place, sources, full, sends, recvs, held, local):
        self.place = place
        self.kinds = sorted(place.lines())
        self.lines, self.over, self.hold, self.keep = [], [], [], []
        self.next = self.begun = self.begun_over = 0
        self.ahead, self.over_ahead = 1, 8
        depth = full.shape[1] // place.count
        per = place.count - 1
        for i, source in enumerate(sources):
            def rows(high, low, i=i):
                at = (high * 2 + low) * depth
                return full.at[i, pl.ds(pl.multiple_of(at, depth), depth)]

            own = rows(place.high, place.low)
            first = i * per
            self.lines.append(
                [
                    send(source(flip(place.pair, pair)), own, sends, recvs, first + k, place.line(step, pair))
                    for k, (step, pair) in enumerate(self.kinds)
                ]
            )
            first += len(self.kinds)
            over = [send(source(place.pair), own, sends, recvs, first, place.across())]
            for k, (step, pair) in enumerate(self.kinds):
                block = rows(place.high_at(-step, pair), place.low)
                over.append(send(block, block, sends, recvs, first + 1 + k, place.across()))
            self.over.append(over)
            self.hold.append(pltpu.make_async_copy(source(place.pair), held.at[i], local.at[0, i]))
            self.keep.append(pltpu.make_async_copy(held.at[i], own, local.at[1, i]))

    def place_own(self):
        for copy in self.hold:
            copy.start()
        for hold, keep in zip(self.hold, self.keep):
            hold.wait()
            keep.start()

    def fill(self):
        while self.begun < min(self.next // len(self.kinds) + self.ahead, len(self.lines)):
            for copy in self.lines[self.begun]:
                copy.start()
            self.begun += 1
        while self.begun_over < min(self.next // len(self.kinds) + self.over_ahead, len(self.lines)):
            self.over[self.begun_over][0].start()
            self.begun_over += 1

    def pump(self, number=1):
        per = len(self.kinds)
        for _ in range(number):
            i, k = divmod(self.next, per)
            if i >= len(self.lines):
                return
            self.lines[i][k].wait_recv()
            self.over[i][k + 1].start()
            self.next += 1
            if self.next % per == 0:
                self.fill()

    def arrive(self, i):
        self.pump(max(0, (i + 1) * len(self.kinds) - self.next))
        for copy in self.over[i]:
            copy.wait_recv()
        self.keep[i].wait()

    def drain(self):
        for copies in self.lines + self.over:
            for copy in copies:
                copy.wait_send()


ANY = pl.BlockSpec(memory_space=pl.ANY)
VMEM = pl.BlockSpec(memory_space=pltpu.VMEM)
DMA = pltpu.SemaphoreType.DMA


FORWARD_ORDER = (
    "k", "k", "k", "k", "k", "k", "xr", "k", "w2", "k", "xf", "t", "k", "k", "t", "k", "t", "q0",
    "k", "k", "q1", "q2", "s", "k", "k", "sf", "rope", "k", "k", "k", "k", "a", "a", "k", "k", "k",
    "k", "t", "f", "s1", "k", "k", "k", "k", "k", "s0", "rl", "k", "T", "k", "N", "k", "k", "R",
    "k", "k", "k", "k", "k", "G", "t", "g0", "k", "k", "k", "k", "g1", "t", "k", "k", "w2", "g2",
    "k", "k", "k", "t", "g3", "k", "t", "k", "t", "t",
)


def forward_kernel(
    count,
    rows_ref, q_ref, k_ref, v_ref, o_ref, gate_ref, up_ref, down_ref, gains_ref, tokens_ref, angles_ref, top_ref,
    full, gains_out, q_rot_out, k_rot_out, v_low_out, q_hat_out, k_hat_out, inv_out,
    normed_out, ainv_out, gate_out, up_out, output, part_out, probs_out, cos_out, sin_out, grad_out, mixed_turned, hidden_turned,
    rows_turned, mid_turned,
    all_rows, all_gains, gains, own_rows, att_w, ffn_w, raw, q_rot, k_rot, v_low, q_hat, k_hat, inv_ref,
    normed_ref, ainv_ref, gate_act, up_act, result, part_gain, probs_ref, cos_ref, sin_ref, mixed_t,
    bias_ref, token_rows, o_turned, down_turned, held,
    mixed, mid, hidden, turning, resid_ref, stats, parts, from_core, from_chips, total,
    wsends, wrecvs, keeps, loads, flushes, xsends, xrecvs, nsends, nrecvs, ssends, srecvs,
    rsends, rrecvs, gsends, grecvs, r2sends, r2recvs, g2sends, g2recvs, turn_sems, tsends, trecvs,
):
    place = Place(count)
    own, width = rows_ref.shape
    tokens = 8 * own
    big = tokens // 2
    cols = q_ref.shape[1] // 2
    heads = cols // HD
    mine = place.slot()
    others = [(place.index + step) % count for step in range(1, count)]

    first_copies = [
        pltpu.make_async_copy(rows_ref, all_rows.at[mine], loads.at[0]),
        pltpu.make_async_copy(gains_ref, all_gains.at[place.index], loads.at[1]),
        pltpu.make_async_copy(rows_ref, own_rows, loads.at[2]),
    ]
    for copy in first_copies:
        copy.start()
    turn_here = o_turned.shape[0] % 128 == 0
    if turn_here:
        narrow = [
            pltpu.make_async_copy(o_ref, ffn_w.at[pl.ds(0, o_ref.shape[0]), pl.ds(cols, cols)], loads.at[3]),
            pltpu.make_async_copy(down_ref, ffn_w.at[pl.ds(0, down_ref.shape[0]), pl.ds(0, cols)], loads.at[4]),
        ]
        for copy in narrow:
            copy.start()
    blocks = [side * 2 + core for core in (0, 1) for side in (0, 1)]
    token_rows[place.pair] = jnp.concatenate(
        [tokens_ref[:, block * own : (block + 1) * own] for block in blocks], axis=1
    )
    greet(
        [{"fsdp": other, "tensor": place.tensor} for other in others]
        + [place.peer(p, c, s) for p, c, s in place.group() if c or s]
    )
    token_copy = send(
        token_rows.at[place.pair], token_rows.at[place.pair], tsends, trecvs, 0, place.peer(pair=1)
    )
    token_copy.start()

    def pieces(ref):
        half = ref.shape[1] // 2

        def source(j):
            return lambda h: ref.at[:, pl.ds(pl.multiple_of(h * half + j * cols, cols), cols)]

        return [source(j) for j in range(half // cols)]

    o_source, down_source = (o_turned, down_turned) if turn_here else (o_ref, down_ref)
    gate_pieces, up_pieces = pieces(gate_ref), pieces(up_ref)
    sources = [pieces(ref)[0] for ref in (q_ref, k_ref, v_ref, o_source)]
    for pair in zip(gate_pieces, up_pieces):
        sources.extend(pair)
    sources.extend(pieces(down_source))
    steps = len(gate_pieces)
    stream = Stream(place, sources, full, wsends, wrecvs, held, keeps)
    rows_gather = Gather(place, all_rows, xsends, xrecvs)
    first_copies[0].wait()
    rows_gather.start()
    if turn_here:
        narrow[0].wait()
        o_turned[...] = jnp.transpose(ffn_w[: o_ref.shape[0], cols : 2 * cols])
        narrow[1].wait()
        for block in range(down_ref.shape[0] // 512):
            at = slice(block * 512, (block + 1) * 512)
            down_turned[:, at] = jnp.transpose(ffn_w[at, :cols])
    stream.fill()
    stream.place_own()
    first_copies[1].wait()
    gain_copies = []
    for i, other in enumerate(others):
        copy = send(
            all_gains.at[place.index],
            all_gains.at[place.index],
            nsends,
            nrecvs,
            i,
            {"fsdp": other, "tensor": place.tensor},
        )
        copy.start()
        gain_copies.append(copy)

    flushed = []

    def flush(src, dst):
        copy = pltpu.make_async_copy(src, dst, flushes.at[len(flushed)])
        copy.start()
        flushed.append(copy)

    token_copy.wait_recv()
    row = lax.broadcasted_iota(jnp.int32, (big, 128), 0)
    natural = row // own % 2 * (2 * own) + row // (2 * own) * own + row % own
    lane = lax.broadcasted_iota(jnp.int32, (big, 128), 1)
    for block in range(2):
        at = slice(block * big, (block + 1) * big)
        angle = over_lanes(token_rows[block, 0:1]) * angles_ref[0:1]
        cos_ref[at] = jnp.cos(angle)
        sin_ref[at] = jnp.sin(angle) * angles_ref[1:2]
        starts = over_lanes(token_rows[block, 1:2])
        for c in range(big // 128):
            lanes = slice(c * 128, (c + 1) * 128)
            first = c * 128
            key = first // own % 2 * (2 * own) + first // (2 * own) * own + first % own + lane
            allowed = (starts == token_rows[block, 1:2, lanes]) & (key <= natural)
            bias_ref[block, :, lanes] = jnp.where(allowed, 0.0, -1e30).astype(BF)
    flush(cos_ref, cos_out)
    flush(sin_ref, sin_out)

    turns = [(all_rows, rows_turned, block) for block in range(width // 512)]
    turns += [(mid, mid_turned, block) for block in range(width // 512)]
    turns += [(hidden, hidden_turned, block) for block in range(hidden.shape[1] // 512)]
    turned_copies = []

    def turn():
        n = len(turned_copies)
        ref, target, block = turns[n]
        if n >= 2:
            turned_copies[-2].wait()
        at = slice(block * 512, (block + 1) * 512)
        part = ref[:, :, at].reshape(tokens, 512) if len(ref.shape) == 3 else ref[:, at]
        turning[n % 2] = jnp.transpose(part)
        copy = pltpu.make_async_copy(turning.at[n % 2], target.at[at], turn_sems.at[n])
        copy.start()
        turned_copies.append(copy)

    def load(i, into):
        stream.arrive(i)
        copy = pltpu.make_async_copy(full.at[i], into, loads.at[5 + i])
        copy.start()
        return copy

    lanes_of = lambda c, number=1: pl.ds(c * cols, number * cols)
    wide = width // gains.shape[1]
    gain_row = lambda first: jnp.concatenate([gains[r : r + 1] for r in range(first, first + wide)], axis=1)

    def rows_arrive():
        rows_gather.finish()
        for copy in gain_copies:
            copy.wait_recv()
        sums = all_gains[0].astype(F32)
        for f in range(1, count):
            sums = sums + all_gains[f].astype(F32)
        gains[...] = sums
        flush(gains, gains_out)

    def project(which):
        load(which, att_w.at[:, lanes_of(which)]).wait()

        @pl.loop(0, 4)
        def _(i):
            m = pl.ds(pl.multiple_of(i * 2 * own, 2 * own), 2 * own)
            left = all_rows[pl.ds(i * 2, 2)].reshape(2 * own, width)
            raw[m, lanes_of(which)] = product(left, att_w[:, lanes_of(which)])

    sum_copies = []

    def squares():
        parts_of = [raw[:, at : at + cols] for at in (0, cols)]
        parts_of = [jnp.sum(part * part, axis=1, keepdims=True) for part in parts_of]
        sum_copies.extend(exchange_sums(place, stats, parts_of, ssends, srecvs))
        v_low[...] = raw[:, 2 * cols :].astype(BF)
        flush(v_low, v_low_out)

    def inverses():
        inverse = lax.rsqrt(finish_sums(stats, sum_copies) / width + NORM_EPS)
        inv_ref[0] = over_lanes(inverse[0:1])
        inv_ref[1] = over_lanes(inverse[1:2])
        flush(inv_ref, inv_out)

    def rotate():
        gain_at = pl.ds(pl.multiple_of(place.pair * cols, cols), cols)

        @pl.loop(0, 8)
        def _(i):
            m = pl.ds(pl.multiple_of(i * own, own), own)
            cosine = cos_ref[m]
            sine = sin_ref[m]
            for which, hat, rot in ((0, q_hat, q_rot), (1, k_hat, k_rot)):
                inv = inv_ref[which, m]
                gain = gains[2 * wide + which : 2 * wide + which + 1, gain_at]
                for h in range(heads):
                    lanes = slice(h * HD, (h + 1) * HD)
                    value = raw[m, which * cols + h * HD : which * cols + (h + 1) * HD] * inv
                    hat[m, lanes] = value
                    value = value * gain[:, lanes]
                    value = value * cosine + pltpu.roll(value, HD // 2, 1) * sine
                    rot[m, lanes] = value.astype(BF)

        for src, dst in ((q_rot, q_rot_out), (k_rot, k_rot_out), (q_hat, q_hat_out), (k_hat, k_hat_out)):
            flush(src, dst)

    scale = HD ** (-0.5)
    quarter = big // 2

    def attend(block, i):
        h = i // 2
        lanes = pl.ds(pl.multiple_of(h * HD, HD), HD)
        q_at = pl.ds(pl.multiple_of(block * big + i % 2 * quarter, quarter), quarter)
        k_at = pl.ds(pl.multiple_of(block * big, big), big)
        b_at = pl.ds(pl.multiple_of(i % 2 * quarter, quarter), quarter)
        scores = product_last(q_rot[q_at, lanes], k_rot[k_at, lanes]) * scale + bias_ref[block, b_at].astype(F32)
        top = jnp.max(scores, axis=1, keepdims=True)
        grown = jnp.exp(scores - top)
        probs = grown / jnp.sum(grown, axis=1, keepdims=True)
        probs = probs.astype(BF)
        probs_ref[block * heads + h, b_at] = probs
        mixed[q_at, lanes] = product(probs, v_low[k_at, lanes]).astype(BF)

    attended = [0]

    def attention():
        pl.loop(0, 2 * heads)(functools.partial(attend, attended[0]))
        attended[0] += 1

    tile = tiles(mixed, att_w, parts, lanes_of(3))
    scatter = Scatter(place, tile, parts, from_core, from_chips, total, rsends, rrecvs, via=True)
    gather = Gather(place, mid, gsends, grecvs)

    def out_first():
        out_load = load(3, att_w.at[:, lanes_of(3)])
        mixed_t[...] = jnp.transpose(mixed[...])
        flush(mixed_t, mixed_turned)
        flush(probs_ref, probs_out)
        rows_gather.drain()
        out_load.wait()
        scatter.first(1)
        scatter.first(0)

    def norm():
        araw = total[...]
        inv = lax.rsqrt(jnp.mean(araw * araw, axis=1, keepdims=True) + NORM_EPS)
        normed = araw * inv
        normed_ref[...] = normed
        ainv_ref[...] = jnp.broadcast_to(inv, (own, 128))
        first_copies[2].wait()
        resid = own_rows[...].astype(F32) + normed * gain_row(0)
        resid_ref[...] = resid
        mid[mine] = resid.astype(BF)
        gather.start()
        for src, dst in ((normed_ref, normed_out), (ainv_ref, ainv_out)):
            flush(src, dst)

    loaded = {}

    def load_step(j):
        if j < steps and j not in loaded:
            at = j % 2 * 2
            loaded[j] = [load(4 + 2 * j + r, ffn_w.at[:, lanes_of(at + r)]) for r in range(2)]

    def gate_and_up(j):
        load_step(j)
        for copy in loaded[j]:
            copy.wait()
        n = slice(j * cols, (j + 1) * cols)

        @pl.loop(0, 4)
        def _(i):
            m = pl.ds(pl.multiple_of(i * 2 * own, 2 * own), 2 * own)
            left = mid[pl.ds(i * 2, 2)].reshape(2 * own, width)
            both = product(left, ffn_w[:, lanes_of(j % 2 * 2, 2)])
            gate = both[:, :cols]
            up = both[:, cols:]
            sig = jax.nn.sigmoid(gate)
            silu = gate * sig
            gate_act[m, n] = up * sig * (1.0 + gate * (1.0 - sig))
            up_act[m, n] = silu
            hidden[m, n] = (silu * up).astype(BF)

        if j == steps - 1:
            for src, dst in ((gate_act, gate_out), (up_act, up_out)):
                flush(src, dst)

    actions = {
        "k": stream.pump,
        "t": turn,
        "xr": rows_gather.relay,
        "xf": rows_arrive,
        "q0": lambda: project(0),
        "q1": lambda: project(1),
        "q2": lambda: project(2),
        "s": squares,
        "sf": inverses,
        "rope": rotate,
        "a": attention,
        "f": out_first,
        "s1": lambda: scatter.second(1),
        "s0": lambda: scatter.second(0),
        "rl": scatter.relay,
        "T": scatter.third,
        "N": norm,
        "R": gather.relay,
        "G": gather.finish,
    }
    for j in range(steps):
        actions["g%d" % j] = functools.partial(gate_and_up, j)
    each = len(stream.kinds) // 3
    for name in FORWARD_ORDER:
        if name == "k":
            stream.pump(each)
        elif name[0] == "w":
            stream.ahead = int(name[1:])
            stream.fill()
        else:
            actions[name]()

    downs = [
        load(i, att_w.at[:, lanes_of(j)]) for j, i in enumerate(range(4 + 2 * steps, len(sources)))
    ]
    for copy in downs:
        copy.wait()
    scatter.drain()
    tile = tiles(hidden, att_w, parts, lanes_of(0, steps))
    again = Scatter(place, tile, parts, from_core, from_chips, total, r2sends, r2recvs)
    again.first(1)
    again.first(0)
    again.second(1)
    again.second(0)
    top = top_ref[...].astype(F32)
    gain = gain_row(wide)
    again.third()
    fraw = total[...]
    inv = lax.rsqrt(jnp.mean(fraw * fraw, axis=1, keepdims=True) + NORM_EPS)
    normed = fraw * inv
    scaled = top * gain
    inner = jnp.mean(scaled * normed, axis=1, keepdims=True)
    all_rows[mine] = (inv * (scaled - normed * inner)).astype(BF)
    last = Gather(place, all_rows, g2sends, g2recvs, split=True)
    last.start()
    result[...] = (resid_ref[...] + normed * gain).astype(BF)
    part_gain[...] = jnp.broadcast_to(jnp.sum(top * normed, axis=0, keepdims=True), part_gain.shape)
    flush(result, output)
    flush(part_gain, part_out)
    last.relay()
    stream.drain()
    gather.drain()
    again.drain()
    for copy in sum_copies + gain_copies + [token_copy]:
        copy.wait_send()
    last.finish()
    flush(all_rows, grad_out)
    last.drain()
    for copy in flushed + turned_copies[-2:]:
        copy.wait()


def run_forward(count, rows, wq, wk, wv, wo, gate, up, down, gains, token_rows, angles, top):
    own, width = rows.shape
    tokens = 8 * own
    half = gate.shape[1] // 2
    cols = wq.shape[1] // 2
    depth = width // count
    pieces = 4 + 3 * (half // cols)
    per = pieces * (count - 1)
    shape = jax.ShapeDtypeStruct
    outs = (
        shape((pieces, width, cols), BF),
        shape(gains.shape, F32),
        shape((tokens, cols), BF), shape((tokens, cols), BF), shape((tokens, cols), BF),
        shape((tokens, cols), F32), shape((tokens, cols), F32), shape((2, tokens, 128), F32),
        shape((own, width), F32), shape((own, 128), F32),
        shape((tokens, half), F32), shape((tokens, half), F32),
        shape((own, width), BF), shape((8, width), F32), shape((2 * cols // HD, tokens // 2, tokens // 2), BF),
        shape((tokens, 128), F32), shape((tokens, 128), F32),
        shape((8, own, width), BF),
        shape((cols, tokens), BF), shape((half, tokens), BF), shape((width, tokens), BF), shape((width, tokens), BF),
    )
    scratch = lambda out: pltpu.VMEM(out.shape, out.dtype)
    return pl.pallas_call(
        functools.partial(forward_kernel, count),
        out_shape=outs,
        in_specs=[ANY] * 9 + [VMEM] * 3,
        out_specs=[ANY] * len(outs),
        scratch_shapes=[
            pltpu.VMEM((8, own, width), BF),
            pltpu.VMEM((count,) + gains.shape, BF),
            scratch(outs[1]),
            pltpu.VMEM((own, width), BF),
            pltpu.VMEM((width, max(4 * cols, half)), BF),
            pltpu.VMEM((width, 4 * cols), BF),
            pltpu.VMEM((tokens, 3 * cols), F32),
            *[scratch(out) for out in outs[2:-5]],
            scratch(outs[-4]),
            pltpu.VMEM((2, tokens // 2, tokens // 2), BF),
            pltpu.VMEM((2,) + token_rows.shape, F32),
            pltpu.VMEM((depth, 2 * cols), BF),
            pltpu.VMEM((depth, 2 * half), BF),
            pltpu.VMEM((pieces, depth, cols), BF),
            pltpu.VMEM((tokens, cols), BF),
            pltpu.VMEM((8, own, width), BF),
            pltpu.VMEM((tokens, half), BF),
            pltpu.VMEM((2, 512, tokens), BF),
            pltpu.VMEM((own, width), F32),
            pltpu.VMEM((8, 8, tokens), F32),
            pltpu.VMEM((8, own, width), BF),
            pltpu.VMEM((4, own, width), BF),
            pltpu.VMEM((3, own, width), BF),
            pltpu.VMEM((own, width), F32),
            DMA((per,)), DMA((per,)), DMA((2, pieces)), DMA((5 + pieces,)), DMA((len(outs),)),
            DMA((9,)), DMA((9,)),
            DMA((count - 1,)), DMA((count - 1,)),
            DMA((7,)), DMA((7,)),
            DMA((7,)), DMA((7,)),
            DMA((9,)), DMA((9,)),
            DMA((7,)), DMA((7,)),
            DMA((9,)), DMA((9,)),
            DMA((2 * (width // 512) + half // 512,)),
            DMA((1,)), DMA((1,)),
        ],
        compiler_params=pltpu.CompilerParams(
            collective_id=0, has_side_effects=True, vmem_limit_bytes=62 * MIB
        ),
        name="forward",
    )(rows, wq, wk, wv, wo, gate, up, down, gains, token_rows, angles, top)


COLUMN_MATRICES = (0, 3)

ORDER = (
    "d", "d", "A", "d", "f1", "p", "f0", "s1", "d", "p", "s0", "d", "p", "d", "d", "p", "d", "d",
    "p", "T", "N", "p", "d", "p", "R", "d", "p", "d", "p", "G", "D", "a", "a", "d", "r", "p", "d",
    "q", "F1", "d", "F0", "d", "p", "d", "S1", "p", "p", "p", "p", "d", "d", "p", "d", "S0", "p",
    "p", "d", "p", "d", "p", "p", "d", "p", "d", "p", "T2", "p",
)


class Collect:
    def __init__(self, place, pieces, depth, gbuf, ybuf, zbuf, ring, came, have, ready, kept, local, ysends,
                 yrecvs, zsends, zrecvs, loads, keeps):
        self.place, self.pieces, self.depth = place, pieces, depth
        columns = [matrix in COLUMN_MATRICES for matrix, _, _, _ in pieces]
        at = [columns[:p].count(columns[p]) for p in range(len(pieces))]
        self.gbuf, self.ybuf, self.zbuf = (
            [bufs[columns[p]].at[at[p]] for p in range(len(pieces))] for bufs in (gbuf, ybuf, zbuf)
        )
        self.ring = ring
        self.came, self.have, self.ready, self.kept = came, have, ready, kept
        self.loads, self.settled = loads, []
        self.made = self.launched = self.summed = 0
        self.flying = []
        self.local, self.over, self.line, self.keep = [], [], [], []
        slot = 0
        for p, (matrix, rows, wide, kind) in enumerate(pieces):
            box = (pl.ds(0, rows), pl.ds(0, wide))
            self.local.append(
                pltpu.make_async_copy(ring.at[(p % 2, slice(None)) + box], self.gbuf[p].at[(slice(None),) + box], local.at[p])
            )
            self.over.append(
                send(
                    self.gbuf[p].at[(1 - place.low,) + box],
                    self.ybuf[p].at[box],
                    ysends,
                    yrecvs,
                    p,
                    place.across(),
                )
            )
            self.keep.append(
                pltpu.make_async_copy(self.gbuf[p].at[(place.low,) + box], have.at[box], loads.at[0])
            )
            if kind == (0, 0):
                self.line.append(None)
                self.settled.append(
                    pltpu.make_async_copy(kept[matrix], self.zbuf[p].at[box], keeps.at[len(self.settled)])
                )
                continue
            self.line.append(
                send(
                    ready.at[(slot % ready.shape[0],) + box],
                    self.zbuf[p].at[box],
                    zsends,
                    zrecvs,
                    p,
                    place.line(*kind),
                )
            )
            slot += 1

    def owner(self, p):
        both = 2 * self.depth
        return pl.ds(pl.multiple_of(self.place.high_at(*self.pieces[p][3]) * both, both), both)

    def make_rows(self, left, right, first):
        p = self.made
        self.launch()
        ring = self.ring.at[p % 2]
        wide = self.pieces[p][2]
        step = 512 if wide % 512 == 0 else 256

        @pl.loop(0, wide // step)
        def _(n):
            lanes = pl.ds(pl.multiple_of(first + n * step, step), step)
            to = pl.ds(pl.multiple_of(n * step, step), step)
            out = product(left[...], right[:, lanes]).astype(BF)
            ring[0, : self.depth, to] = out[: self.depth]
            ring[1, : self.depth, to] = out[self.depth :]

        self.local[p].start()
        self.made = p + 1

    def make_columns(self, left, right):
        p = self.made
        self.launch()
        ring = self.ring.at[p % 2]
        _, rows, wide, _ = self.pieces[p]
        number = left.shape[0] // rows
        pitch = wide // number
        tokens = right.shape[0] * right.shape[1]
        cols = right[:, :, self.owner(p)].reshape(tokens, 2 * self.depth)
        together = 2 if number % 2 == 0 else 1
        for c in range(0, number, together):
            out = product(left[c * rows : (c + together) * rows], cols).astype(BF)
            for r in range(together):
                for low in (0, 1):
                    ring[low, :rows, (c + r) * pitch : (c + r) * pitch + self.depth] = out[
                        r * rows : (r + 1) * rows, low * self.depth : (low + 1) * self.depth
                    ]
        self.local[p].start()
        self.made = p + 1

    def launch(self):
        while self.launched < self.made:
            self.local[self.launched].wait()
            self.over[self.launched].start()
            self.launched += 1

    def pump(self, number=1):
        self.launch()
        for _ in range(number):
            p = self.summed
            if p >= self.made:
                return
            matrix, rows, wide, kind = self.pieces[p]
            box = (slice(0, rows), slice(0, wide))
            self.keep[p].start()
            self.over[p].wait_recv()
            came = pltpu.make_async_copy(
                self.ybuf[p].at[pl.ds(0, rows), pl.ds(0, wide)],
                self.came.at[pl.ds(0, rows), pl.ds(0, wide)],
                self.loads.at[2],
            )
            came.start()
            self.keep[p].wait()
            came.wait()
            total = self.came[box].astype(F32) + self.have[box].astype(F32)
            if kind == (0, 0):
                self.kept[matrix][...] = total.astype(BF)
                self.settled[matrix].start()
            else:
                slots = self.ready.shape[0]
                if len(self.flying) >= slots:
                    self.flying[-slots].wait_send()
                self.ready[(len(self.flying) % slots,) + box] = total.astype(BF)
                self.line[p].start()
                self.flying.append(self.line[p])
            self.summed = p + 1

    def drain(self):
        for copy in self.over:
            copy.wait_send()
        for copy in self.flying[-self.ready.shape[0] :]:
            copy.wait_send()
        for copy in self.line:
            if copy is not None:
                copy.wait_recv()
        for copy in self.settled:
            copy.wait()


def backward_kernel(
    count, pieces,
    gffn_in, hidden_in, gate_in, up_in, mid_in, rows_in, full, mixed_in, q_in, k_in, v_in, qh_in, kh_in, inv_in,
    cos_in, sin_in, probs_in, normed_ref, ainv_ref, top_ref, gains_ref, pgain_ref,
    grad_rows, gain_sums,
    gbuf_r, gbuf_c, ybuf_r, ybuf_c, zbuf_r, zbuf_c,
    rows_a, rows_c, hidden, acts, floats, weights, parts, from_core, from_chips, total, resid, turned, ring,
    came, have, ready, kept0, kept1, kept2, kept3, kept4, kept5,
    mixed, q_rot, k_rot, v_low, q_hat, k_hat, inv, cos_ref, sin_ref, probs_ref, datt, dqkv, stats, part_sums, inner_sums, side_sums, all_sums,
    big_loads, loads, local, ysends, yrecvs, zsends, zrecvs, rsends, rrecvs, r2sends, r2recvs, gsends, grecvs,
    ssends, srecvs, xsends, xrecvs, fsends, frecvs, keeps,
):
    place = Place(count)
    own, width = top_ref.shape
    tokens = 8 * own
    big = tokens // 2
    cols = mixed.shape[0]
    heads = cols // HD
    steps = hidden.shape[0] // cols
    depth = width // count
    others = [(place.index + step) % count for step in range(1, count)]
    tensor_peers = [(0, 1), (1, 0), (1, 1)]

    used = [0]

    def load(src, into):
        copy = pltpu.make_async_copy(src, into, big_loads.at[used[0]])
        used[0] += 1
        copy.start()
        return copy

    def chunk(ref, j):
        return ref.at[:, pl.ds(j * cols, cols)]

    rows_load = load(gffn_in, rows_a)
    hidden_load = load(hidden_in, hidden)
    firsts = [
        [
            load(full.at[4 + 2 * steps + j], chunk(weights, j)),
            load(chunk(gate_in, j), floats.at[2 * (j % 2)]),
            load(chunk(up_in, j), floats.at[2 * (j % 2) + 1]),
        ]
        for j in range(min(2, steps))
    ]
    for j in range(2, steps):
        firsts.append([load(full.at[4 + 2 * steps + j], chunk(weights, j))])
    greet(
        [{"fsdp": other, "tensor": place.tensor} for other in others]
        + [place.peer(p, c, s) for p, c, s in place.group() if c or s]
    )
    kept = [kept0, kept1, kept2, kept3, kept4, kept5]
    collect = Collect(
        place, pieces, depth, (gbuf_r, gbuf_c), (ybuf_r, ybuf_c), (zbuf_r, zbuf_c), ring, came, have, ready, kept, local,
        ysends, yrecvs, zsends, zrecvs, loads, keeps,
    )
    number = len(place.lines()) + 1

    wanted = [(mid_in, number + 2 * k) for k in range(number)] + [
        (rows_in, (4 + turn) * number + k) for turn in range(2) for k in range(number)
    ]
    blocks = []

    def next_block():
        i = len(blocks)
        if i < len(wanted):
            ref, p = wanted[i]
            blocks.append(load(ref.at[collect.owner(p)], turned.at[i % 2]))

    next_block()
    next_block()
    waited = set()

    def once(*copies):
        for copy in copies:
            if id(copy) not in waited:
                waited.add(id(copy))
                copy.wait()

    def make_down():
        once(rows_load, hidden_load)
        collect.make_columns(hidden, rows_a)

    def make_rows(i, right, first, last):
        once(blocks[i])
        collect.make_rows(turned.at[i % 2], right, first)
        if last:
            next_block()

    makes = [make_down] * number
    for k in range(number):
        makes.append(functools.partial(make_rows, k, acts, 0, False))
        makes.append(functools.partial(make_rows, k, acts, steps * cols, True))
    def make_out():
        once(*late["rest"])
        collect.make_columns(mixed, rows_c)

    makes += [make_out] * number
    for turn, first in ((1, 2 * cols), (2, 0)):
        for k in range(number):
            makes.append(functools.partial(make_rows, turn * number + k, dqkv, first, True))

    late = {}

    def gate_and_up():
        once(rows_load)
        for j in range(steps):
            once(*firsts[j])
            at = 2 * (j % 2)

            @pl.loop(0, 2)
            def _(i):
                m = pl.ds(pl.multiple_of(i * big, big), big)
                left = rows_a[pl.ds(i * 4, 4)].reshape(big, width)
                grad = product(left, weights[:, j * cols : (j + 1) * cols])
                acts[m, 2 * j * cols : (2 * j + 1) * cols] = (grad * floats[at, m]).astype(BF)
                acts[m, (2 * j + 1) * cols : (2 * j + 2) * cols] = (grad * floats[at + 1, m]).astype(BF)

            if j + 2 < steps:
                firsts[j + 2] += [
                    load(chunk(gate_in, j + 2), floats.at[at]),
                    load(chunk(up_in, j + 2), floats.at[at + 1]),
                ]
        late["ffn"] = [load(full.at[4 + c], chunk(weights, c)) for c in range(2 * steps)]
        late["rest"] = [
            load(src, into)
            for src, into in (
                (mixed_in, mixed), (q_in, q_rot), (k_in, k_rot), (v_in, v_low), (qh_in, q_hat), (kh_in, k_hat),
                (inv_in, inv), (cos_in, cos_ref), (sin_in, sin_ref), (probs_in, probs_ref),
            )
        ]

    tile = tiles(acts, weights, parts, pl.ds(0, acts.shape[1]))
    scatter = Scatter(place, tile, parts, from_core, from_chips, total, rsends, rrecvs, via=True)
    tile = tiles(dqkv, weights, parts, pl.ds(0, 3 * cols))
    again = Scatter(place, tile, parts, from_core, from_chips, total, r2sends, r2recvs, via=True)
    gather = Gather(place, rows_c, gsends, grecvs)
    wide = width // gains_ref.shape[1]
    lanes_per = gains_ref.shape[1]
    cut = lambda row: [row[:, r * lanes_per : (r + 1) * lanes_per] for r in range(wide)]
    side_copies, inner_copies, all_copies = [], [], []

    def first(pair):
        once(*late["ffn"])
        scatter.first(pair)

    def second(pair):
        scatter.second(pair)
        if not pair:
            scatter.relay()
            late["att"] = [load(full.at[c], chunk(weights, c)) for c in range(4)]

    def norm():
        normed = normed_ref[...]
        gain = jnp.concatenate([gains_ref[r : r + 1] for r in range(wide)], axis=1)
        grad = top_ref[...].astype(F32) + total[...]
        resid[...] = grad
        part_gain = jnp.sum(grad * normed, axis=0, keepdims=True)
        scaled = grad * gain
        inner = jnp.mean(scaled * normed, axis=1, keepdims=True)
        rows_c[place.slot()] = (ainv_ref[:, :1] * (scaled - normed * inner)).astype(BF)
        gather.start()
        side_sums[place.tensor] = jnp.concatenate(cut(part_gain) + cut(pgain_ref[0:1]), axis=0)
        for i, (c, s) in enumerate(tensor_peers):
            copy = send(
                side_sums.at[place.tensor], side_sums.at[place.tensor], xsends, xrecvs, i, place.peer(0, c, s)
            )
            copy.start()
            side_copies.append(copy)

    def out_back():
        once(*late["att"], *late["rest"])

        @pl.loop(0, 2)
        def _(i):
            m = pl.ds(pl.multiple_of(i * big, big), big)
            left = rows_c[pl.ds(i * 4, 4)].reshape(big, width)
            datt[m] = product(left, weights[:, 3 * cols : 4 * cols]).astype(BF)

    scale = HD ** (-0.5)
    quarter = big // 2

    def attend(block, h):
        lanes = pl.ds(pl.multiple_of(h * HD, HD), HD)
        k_at = pl.ds(pl.multiple_of(block * big, big), big)
        keys = k_rot[k_at, lanes]
        values = v_low[k_at, lanes]
        for half in range(2):
            q_at = pl.ds(pl.multiple_of(block * big + half * quarter, quarter), quarter)
            queries = q_rot[q_at, lanes]
            grads = datt[q_at, lanes]
            low = probs_ref[block * heads + h, half * quarter : (half + 1) * quarter]
            probs = low.astype(F32)
            dprobs = product_last(grads, values)
            inner = jnp.sum(probs * dprobs, axis=1, keepdims=True)
            dscores = (probs * (dprobs - inner)).astype(BF)
            floats[0, q_at, lanes] = product(dscores, keys) * scale
            dkeys = product_first(dscores, queries) * scale
            dvalues = product_first(low, grads)
            if half:
                floats[1, k_at, lanes] += dkeys
                floats[2, k_at, lanes] += dvalues
            else:
                floats[1, k_at, lanes] = dkeys
                floats[2, k_at, lanes] = dvalues

    attended = [0]

    def attention():
        pl.loop(0, heads)(functools.partial(attend, attended[0]))
        m = pl.ds(attended[0] * big, big)
        dqkv[m, 2 * cols :] = floats[2, m].astype(BF)
        attended[0] += 1

    def rotate_back():
        gain_at = pl.ds(pl.multiple_of(place.pair * cols, cols), cols)
        norm_gains = [gains_ref[2 * wide + which : 2 * wide + which + 1, gain_at] for which in (0, 1)]
        mine = place.slot()
        stats[mine] = jnp.zeros(stats.shape[1:], F32)
        part_sums[...] = jnp.zeros(part_sums.shape, F32)

        @pl.loop(0, 8)
        def _(i):
            m = pl.ds(pl.multiple_of(i * own, own), own)
            cosine = cos_ref[m]
            sine = sin_ref[m]
            for which, hat in ((0, q_hat), (1, k_hat)):
                inner = 0.0
                for h in range(heads):
                    lanes = slice(h * HD, (h + 1) * HD)
                    value = floats[which, m, lanes]
                    value = value * cosine - pltpu.roll(value, HD // 2, 1) * sine
                    weighted = value * hat[m, lanes]
                    part_sums[which, :, lanes] += jnp.sum(weighted.reshape(own // 8, 8, HD), axis=0)
                    part = norm_gains[which][:, lanes]
                    inner = inner + jnp.sum(weighted * part, axis=1, keepdims=True)
                    floats[which, m, lanes] = value * part
                stats[mine, which : which + 1, m] = jnp.transpose(jnp.broadcast_to(inner, (own, 128)))[0:1]

        inner_copies.extend(exchange_rows(place, stats, ssends, srecvs))
        for copy in side_copies:
            copy.wait_recv()
        side = side_sums[0]
        for t in range(1, side_sums.shape[0]):
            side = side + side_sums[t]
        gain_rows = [jnp.sum(part_sums[w], axis=0, keepdims=True) for w in (0, 1)]
        upper = place.pair == 1
        gain_rows = [
            jnp.concatenate([jnp.where(upper, 0.0, row), jnp.where(upper, row, 0.0)], axis=1) for row in gain_rows
        ]
        spare = jnp.zeros((all_sums.shape[1] - 2 * wide - 2, lanes_per), F32)
        all_sums[place.index] = jnp.concatenate([side] + gain_rows + [spare], axis=0)
        for i, other in enumerate(others):
            copy = send(
                all_sums.at[place.index], all_sums.at[place.index], fsends, frecvs, i,
                {"fsdp": other, "tensor": place.tensor},
            )
            copy.start()
            all_copies.append(copy)

    def query_key():
        inner_sums[...] = finish_sums(stats, inner_copies) / width

        @pl.loop(0, 8)
        def _(i):
            m = pl.ds(pl.multiple_of(i * own, own), own)
            for which, hat in ((0, q_hat), (1, k_hat)):
                inner = over_lanes(inner_sums[which : which + 1, m])
                for h in range(heads):
                    lanes = slice(h * HD, (h + 1) * HD)
                    value = inv[which, m] * (floats[which, m, lanes] - hat[m, lanes] * inner)
                    dqkv[m, which * cols + h * HD : which * cols + (h + 1) * HD] = value.astype(BF)

    def first_again(pair):
        if pair:
            scatter.drain()
        again.first(pair)

    def second_again(pair):
        again.second(pair)
        if not pair:
            again.relay()

    grad_copies = []

    def third_again():
        again.third()
        total[...] += resid[...]
        grad_copies.append(load(total, grad_rows))

    actions = {
        "A": gate_and_up,
        "f1": lambda: first(1),
        "f0": lambda: first(0),
        "s1": lambda: second(1),
        "s0": lambda: second(0),
        "T": scatter.third,
        "N": norm,
        "R": gather.relay,
        "G": gather.finish,
        "D": out_back,
        "a": attention,
        "r": rotate_back,
        "q": query_key,
        "F1": lambda: first_again(1),
        "F0": lambda: first_again(0),
        "S1": lambda: second_again(1),
        "S0": lambda: second_again(0),
        "T2": third_again,
    }
    each = number // 4
    for name in ORDER:
        if name == "d":
            for _ in range(each):
                makes.pop(0)()
        elif name == "p":
            collect.pump(each)
        else:
            actions[name]()
    for copy in all_copies:
        copy.wait_recv()
    sums = all_sums[0]
    for f in range(1, count):
        sums = sums + all_sums[f]
    gain_sums[...] = sums
    for copy in grad_copies:
        copy.wait()
    collect.drain()
    again.drain()
    gather.drain()
    for copy in inner_copies + side_copies + all_copies:
        copy.wait_send()


def list_pieces(count, depth, cols, half):
    kinds = line_kinds(count) + [(0, 0)]
    pitch = max(depth, 128)
    sizes = [
        (cols, half // cols * pitch), (depth, half), (depth, half), (cols, pitch), (depth, cols), (depth, 2 * cols),
    ]
    order = [[0], [1, 2], [3], [4], [5]]
    return sizes, [(m,) + sizes[m] + (kind,) for group in order for kind in kinds for m in group]


def settle_kernel(
    pieces, zbuf_r, zbuf_c, grad_in, out_in,
    out_q, out_k, out_v, out_o, out_gate, out_up, out_down, grad_out, out_out,
    boxes_r, boxes_c, grad_held, out_held, stage0, stage1, stage2, stage3, stage4, stage5, loads, stores, copies,
):
    stages = [stage0, stage1, stage2, stage3, stage4, stage5]
    whole = []
    for i, (src, held_here, dst) in enumerate(((grad_in, grad_held, grad_out), (out_in, out_held, out_out))):
        into = pltpu.make_async_copy(src, held_here, copies.at[i])
        into.start()
        whole.append((into, pltpu.make_async_copy(held_here, dst, copies.at[2 + i])))
    pair = lax.axis_index("fsdp") // 2 % 2
    held, count = [], [0, 0]
    for p, (matrix, _, _, _) in enumerate(pieces):
        column = matrix in COLUMN_MATRICES
        at = count[column]
        count[column] += 1
        zbuf, boxes = (zbuf_c, boxes_c) if column else (zbuf_r, boxes_r)
        _, rows, wide, _ = pieces[p]
        box = (pl.ds(0, rows), pl.ds(0, wide))
        copy = pltpu.make_async_copy(zbuf.at[(at,) + box], boxes.at[(at,) + box], loads.at[p])
        copy.start()
        held.append((copy, boxes, at))
    for into, back in whole:
        into.wait()
        back.start()
    cols = out_q.shape[1] // 2
    steps = out_gate.shape[1] // 2 // cols
    both = [(ref, j * cols) for j in range(steps) for ref in (out_gate, out_up)]
    groups = [
        [(out_down, None)] * steps,
        both[:steps],
        both[steps:],
        [(out_o, None)],
        [(out_v, 0)],
        [(out_q, 0), (out_k, 0)],
    ]
    sent = []
    for matrix, targets in enumerate(groups):
        for p, (m, _, _, _) in enumerate(pieces):
            if m == matrix:
                held[p][0].wait()
        stage = stages[matrix]
        rows, wide = stage.shape[1:]
        step = min(rows, 64)

        @pl.loop(0, rows // step)
        def _(i):
            at = pl.ds(pl.multiple_of(i * step, step), step)
            sums = [None, None]
            for p, (m, _, _, kind) in enumerate(pieces):
                if m != matrix:
                    continue
                _, boxes, index = held[p]
                part = boxes[index, at, :wide].astype(F32)
                which = kind[1]
                sums[which] = part if sums[which] is None else sums[which] + part
            stage[0, at] = sums[0]
            stage[1, at] = sums[1]

        pitch = wide // len(targets)
        for r in (0, 1):
            half = flip(pair, r)
            for c, (ref, at) in enumerate(targets):
                src = stage.at[r, :, pl.ds(c * pitch, pitch)]
                if at is None:
                    start = half * (ref.shape[0] // 2) + c * rows
                    dst = ref.at[pl.ds(pl.multiple_of(start, rows), rows)]
                else:
                    start = half * (ref.shape[1] // 2) + at
                    dst = ref.at[:, pl.ds(pl.multiple_of(start, pitch), pitch)]
                copy = pltpu.make_async_copy(src, dst, stores.at[len(sent)])
                copy.start()
                sent.append(copy)
    for copy in sent + [back for _, back in whole]:
        copy.wait()


def run_settle(count, cols, half, zbuf_r, zbuf_c, grad, output):
    width = grad.shape[1]
    depth = width // count
    sizes, pieces = list_pieces(count, depth, cols, half)
    pitch = max(depth, 128)
    shape = jax.ShapeDtypeStruct
    small = shape((depth, 2 * cols), F32)
    large = shape((depth, 2 * half), F32)
    outs = (
        small, small, small, shape((2 * cols, pitch), F32),
        large, large, shape((2 * half, pitch), F32),
        shape(grad.shape, grad.dtype), shape(output.shape, output.dtype),
    )
    return pl.pallas_call(
        functools.partial(settle_kernel, pieces),
        out_shape=outs,
        in_specs=[ANY] * 4,
        out_specs=[ANY] * len(outs),
        scratch_shapes=[
            pltpu.VMEM(zbuf_r.shape, BF),
            pltpu.VMEM(zbuf_c.shape, BF),
            pltpu.VMEM(grad.shape, grad.dtype),
            pltpu.VMEM(output.shape, output.dtype),
            *[pltpu.VMEM((2,) + size, F32) for size in sizes],
            DMA((len(pieces),)), DMA((64,)), DMA((4,)),
        ],
        compiler_params=pltpu.CompilerParams(vmem_limit_bytes=62 * MIB),
        name="settle",
    )(zbuf_r, zbuf_c, grad, output)


def run_backward(
    count, gffn, hidden, gate, up, mid, rows, full, mixed, q_rot, k_rot, v_low, q_hat, k_hat, inv, cosine, sine, probs,
    normed, ainv, top, gains, part_gain,
):
    own, width = top.shape
    tokens = 8 * own
    cols = mixed.shape[0]
    half = hidden.shape[0]
    depth = width // count
    steps = half // cols
    pitch = max(depth, 128)
    kinds = line_kinds(count) + [(0, 0)]
    sizes, pieces = list_pieces(count, depth, cols, half)
    number = len(pieces)
    kinds_of = ((4 * len(kinds), sizes[1]), (2 * len(kinds), sizes[0]))
    box = (max(depth, cols), half)
    shape = jax.ShapeDtypeStruct
    outs = (
        shape((own, width), F32),
        shape(gains.shape, F32),
        *[shape((n,) + lead + size, BF) for lead in ((2,), (), ()) for n, size in kinds_of],
    )
    like = lambda array: pltpu.VMEM(array.shape, array.dtype)
    return pl.pallas_call(
        functools.partial(backward_kernel, count, pieces),
        out_shape=outs,
        in_specs=[ANY] * 17 + [VMEM] * 5,
        out_specs=[ANY, VMEM] + [ANY] * 6,
        scratch_shapes=[
            like(gffn), like(gffn), like(hidden),
            pltpu.VMEM((tokens, 2 * half), BF),
            pltpu.VMEM((4, tokens, cols), F32),
            pltpu.VMEM((width, 2 * half), BF),
            pltpu.VMEM((8, own, width), BF),
            pltpu.VMEM((4, own, width), BF),
            pltpu.VMEM((3, own, width), BF),
            pltpu.VMEM((own, width), F32),
            pltpu.VMEM((own, width), F32),
            pltpu.VMEM((2, 2 * depth, tokens), BF),
            pltpu.VMEM((2, 2) + box, BF),
            pltpu.VMEM(box, BF),
            pltpu.VMEM(box, BF),
            pltpu.VMEM((6,) + box, BF),
            *[pltpu.VMEM(size, BF) for size in sizes],
            like(mixed), like(q_rot), like(k_rot), like(v_low), like(q_hat), like(k_hat), like(inv),
            like(cosine), like(sine), like(probs),
            pltpu.VMEM((tokens, cols), BF),
            pltpu.VMEM((tokens, 3 * cols), BF),
            pltpu.VMEM((8, 8, tokens), F32),
            pltpu.VMEM((2, 8, cols), F32),
            pltpu.VMEM((8, tokens), F32),
            pltpu.VMEM((4, 2 * width // gains.shape[1], gains.shape[1]), F32),
            pltpu.VMEM((count,) + gains.shape, F32),
            DMA((64 + 3 * len(kinds),)), DMA((3,)), DMA((number,)),
            DMA((number,)), DMA((number,)),
            DMA((number,)), DMA((number,)),
            DMA((7,)), DMA((7,)),
            DMA((7,)), DMA((7,)),
            DMA((9,)), DMA((9,)),
            DMA((7,)), DMA((7,)),
            DMA((3,)), DMA((3,)),
            DMA((count - 1,)), DMA((count - 1,)),
            DMA((6,)),
        ],
        compiler_params=pltpu.CompilerParams(
            collective_id=1, has_side_effects=True, vmem_limit_bytes=63 * MIB
        ),
        name="backward",
    )(
        gffn, hidden, gate, up, mid, rows, full, mixed, q_rot, k_rot, v_low, q_hat, k_hat, inv, cosine, sine, probs,
        normed, ainv, top, gains, part_gain,
    )


def local(
    inputs,
    seg_ids,
    positions,
    w_query,
    w_key,
    w_value,
    w_out,
    query_gain,
    key_gain,
    attn_gain,
    w_gate,
    w_up,
    w_down,
    ffn_gain,
    out_grad,
    count,
    tensor,
):
    index = lax.axis_index("fsdp")
    own_rows, width = inputs.shape
    group_rows = seg_ids.shape[0]
    depth = width // count

    heads_here, part = query_gain.shape
    heads_half = heads_here // 2
    cols = heads_half * HD
    sizes = heads_here * part

    def placed(values, copies):
        size = values.shape[-1]
        here = jnp.arange(size * count, dtype=jnp.int32) // size == index
        return jnp.where(here, jnp.tile(values, copies), 0).reshape(-1, heads_here * HD)

    packed = jnp.concatenate(
        [
            placed(attn_gain, count),
            placed(ffn_gain, count),
            placed(jnp.concatenate([query_gain, key_gain]), (1, count)),
        ]
    )
    packed = jnp.pad(packed, ((0, -packed.shape[0] % 16), (0, 0)))

    token_rows = jnp.pad(jnp.stack([positions, seg_ids]).astype(F32), ((0, 6), (0, 0)))
    freq = np.float32(ROPE_THETA) ** (-(np.arange(HD // 2, dtype=np.float32) * 2) / np.float32(HD))
    angles = np.zeros((8, HD), np.float32)
    angles[0] = np.concatenate([freq, freq])
    angles[1] = np.concatenate([-np.ones(HD // 2), np.ones(HD // 2)])
    turned = depth % 128 != 0

    (
        full, gains, query_rot, key_rot, value_low, query_hat, key_hat, invs, attn_normed, attn_inv, gate_raw, up_raw,
        output, partial_ffn_gain, probs, cosine, sine, rows_grad_ffn, mixed_low, hidden_low, all_rows, rows_mid,
    ) = run_forward(
        count, inputs, w_query, w_key, w_value, w_out.T if turned else w_out, w_gate, w_up,
        w_down.T if turned else w_down, packed, token_rows, angles, out_grad,
    )
    wide = width // gains.shape[1]
    (
        grad_rows, gain_sums, _, _, _, _, zbuf_r, zbuf_c,
    ) = run_backward(
        count, rows_grad_ffn, hidden_low, gate_raw, up_raw, rows_mid, all_rows, full, mixed_low, query_rot,
        key_rot, value_low, query_hat, key_hat, invs, cosine, sine, probs, attn_normed, attn_inv,
        out_grad, gains, partial_ffn_gain,
    )

    (
        sum_query, sum_key, sum_value, sum_out, sum_gate, sum_up, sum_down, grad_inputs, output,
    ) = run_settle(count, cols, hidden_low.shape[0], zbuf_r, zbuf_c, grad_rows, output)

    def own_gain(row):
        return lax.dynamic_slice_in_dim(gain_sums[row * wide : (row + 1) * wide].reshape(-1), index * depth, depth)

    def own_head_gain(row):
        values = gain_sums[2 * wide + row].reshape(heads_here, HD)
        return lax.dynamic_slice_in_dim(values, index * part, part, 1)

    return (
        output,
        grad_inputs,
        sum_query,
        sum_key,
        sum_value,
        sum_out[:, :depth],
        own_head_gain(0),
        own_head_gain(1),
        own_gain(0),
        sum_gate,
        sum_up,
        sum_down[:, :depth],
        own_gain(1),
    )


def solution(mesh):
    count = mesh.shape["fsdp"]
    tensor = mesh.shape["tensor"]
    tokens = P(("fsdp", "tensor"), None)
    rows = P("fsdp", "tensor")
    columns = P("tensor", "fsdp")
    line = P("fsdp")

    def body(*arrays):
        return local(*arrays, count=count, tensor=tensor)

    return jax.shard_map(
        body,
        mesh=mesh,
        in_specs=(
            tokens, line, line, rows, rows, rows, columns, columns, columns, line,
            rows, rows, columns, line, tokens,
        ),
        out_specs=(
            tokens, tokens, rows, rows, rows, columns, columns, columns, line,
            rows, rows, columns, line,
        ),
        check_vma=False,
    )
```
